128 devices in a mesh: section: 2 (over core), batch: 64 (over z, y, x).
Axes of the slice: x: 4, y: 4, z: 4, core: 2. Of those that a mesh axis runs over, the one named last changes fastest.
Arguments:
- tokens: bfloat16 [2, 64, 128, 1024], P(None, 'batch'), may hold values from -6 to 6
- pixels: bfloat16 [2, 64, 48, 4, 128], P(None, 'batch'), may hold values from -6 to 6
- segments: int32 [2, 64, 128], P(None, 'batch'), may hold values from 0 to 3, never falling along the last dimension, each value on 1 to 64 neighbouring positions
- embed_weight: bfloat16 [2, 48, 4, 1024], P('section'), may hold values from -3 to 3
- var_embed: bfloat16 [2, 48, 1024], P('section'), may hold values from -6 to 6
- var_query: bfloat16 [2, 1024], P('section'), may hold values from -6 to 6
- query_weight: bfloat16 [2, 1024, 1024], P('section'), may hold values from -0.1875 to 0.1875
- key_weight: bfloat16 [2, 1024, 1024], P('section'), may hold values from -0.1875 to 0.1875
- value_weight: bfloat16 [2, 1024, 1024], P('section'), may hold values from -0.1875 to 0.1875
- pool_weight: bfloat16 [2, 1024, 1024], P('section'), may hold values from -0.375 to 0.375
- first_gain: bfloat16 [2, 1024], P('section'), may hold values from 0.5 to 1.5
- project_in: bfloat16 [2, 1024, 3072], P('section'), may hold values from -0.1875 to 0.1875
- project_out: bfloat16 [2, 1024, 1024], P('section'), may hold values from -0.5 to 0.5
- second_gain: bfloat16 [2, 1024], P('section'), may hold values from 0.5 to 1.5
- up_weight: bfloat16 [2, 1024, 4096], P('section'), may hold values from -0.1875 to 0.1875
- up_bias: bfloat16 [2, 4096], P('section'), may hold values from -3 to 3
- down_weight: bfloat16 [2, 4096, 1024], P('section'), may hold values from -0.09375 to 0.09375
- down_bias: bfloat16 [2, 1024], P('section'), may hold values from -3 to 3
- cotangent: bfloat16 [2, 64, 128, 1024], P(None, 'batch'), may hold values from -16 to 16
Outputs:
- layer_outputs: bfloat16 [2, 2, 64, 128, 1024], P('section', None, 'batch')
- input_grads: float32 [2, 2, 64, 128, 1024], P('section', None, 'batch')
- grad_embed: float32 [2, 48, 4, 1024], P('section', None, None, 'batch')
- grad_var_embed: float32 [2, 48, 1024], P('section', None, 'batch')
- grad_var_query: float32 [2, 1024], P('section', 'batch')
- grad_query_weight: float32 [2, 1024, 1024], P('section', 'batch')
- grad_key_weight: float32 [2, 1024, 1024], P('section', 'batch')
- grad_value_weight: float32 [2, 1024, 1024], P('section', 'batch')
- grad_pool_weight: float32 [2, 1024, 1024], P('section', 'batch')
- grad_first_gain: float32 [2, 1024], P('section', 'batch')
- grad_project_in: float32 [2, 1024, 3072], P('section', 'batch')
- grad_project_out: float32 [2, 1024, 1024], P('section', 'batch')
- grad_second_gain: float32 [2, 1024], P('section', 'batch')
- grad_up_weight: float32 [2, 1024, 4096], P('section', 'batch')
- grad_up_bias: float32 [2, 4096], P('section', 'batch')
- grad_down_weight: float32 [2, 4096, 1024], P('section', None, 'batch')
- grad_down_bias: float32 [2, 1024], P('section', 'batch')
The draws below stay inside these ranges and needn't reach their ends.
Inputs may be any that keep to these rules, and one draw needn't show every extreme that they name: `segments`: segment numbers of a row never fall; a patch attends only to patches of its row with the same number.
All inputs are finite; a program needn't handle non-finite values.
Results may differ from the reference program's by a relative error of at most 0.02.
Values may be sent and summed in bfloat16 or wider, within the bound.
No kernel may reach another device: no remote copies, remote signals or barrier semaphores. Data moves between devices by JAX's collectives and lax.ppermute only.
A program may use at most 512 MiB of HBM per device.

```python
import math
import jax
import jax.numpy as jnp
import numpy as np
from jax import lax

D = 1024
HEADS = 16
HEAD = 64
FF = 4096
VARS = 48
PIX = 4
SEQ = 128
SEGS = 4
MICRO = 2
ROWS = 64
LAYERS = 2


def strengthened(array, rng, source, target, blocks, factor):
    owner, partner = [(jnp.arange(array.shape[dim]) // (array.shape[dim] // blocks)).reshape([-1 if axis == dim else 1 for axis in range(array.ndim)]) for dim in (source, target)]
    chosen = jax.random.permutation(rng, blocks)[partner]
    strong = (owner == chosen) | (owner == (partner + blocks // 2) % blocks)
    return jnp.where(strong, factor * array, array)


def levels(key, extent, cuts, least, high):
    loudness = 1.0
    for dim, shards_of in cuts:
        draws = jax.random.uniform(jax.random.fold_in(jax.random.fold_in(key, 6), dim), (shards_of,), jnp.float32, least / len(cuts), high / len(cuts))
        loudness = loudness * jnp.repeat(jnp.exp(draws), extent[dim] // shards_of).reshape((-1,) + (1,) * (len(extent) - 1 - dim))
    return loudness


def split_up(number_of, total, limit, skew):
    portions = [(1 << 20) // math.isqrt(rank ** skew) + 1 for rank in range(2, number_of + 1)]
    surplus, holding = total - limit - (number_of - 1), [1] * (number_of - 1)
    while surplus > 0:
        free = [i for i in range(number_of - 1) if holding[i] < limit]
        pool, budget = sum([portions[i] for i in free]), surplus
        for i in free:
            addition = min(limit - holding[i], max(1, budget * portions[i] // pool), surplus)
            holding[i] = holding[i] + addition
            surplus = surplus - addition
    return np.array([limit] + holding)


def ragged(own_key, amount, total, reach, slope):
    if amount == 2:
        one = jax.random.randint(own_key, (), max(1, total - reach), min(reach, total - 1) + 1)
        return jnp.stack([one, total - one])
    lengths = jnp.asarray(split_up(amount, total, reach, slope), jnp.int32)
    couples = (amount - 1) // 2
    donor, receiver = lengths[1:1 + 2 * couples:2], lengths[2:2 + 2 * couples:2]
    slack = jnp.minimum(donor - 1, reach - receiver)
    shifted = jax.random.randint(jax.random.fold_in(own_key, 1), (couples,), 0, 1 << 20) % (slack + 1)
    lengths = lengths.at[1:1 + 2 * couples:2].set(donor - shifted).at[2:2 + 2 * couples:2].set(receiver + shifted)
    return lengths[jax.random.permutation(jax.random.fold_in(own_key, 2), amount)]


def gaussian(own_key, shape, deviation, limit, cuts=(), held_as=jnp.bfloat16):
    entries = jax.random.normal(own_key, shape, jnp.float32) * deviation
    if len(cuts) > 0:
        entries = levels(own_key, shape, cuts, -0.22, 0.18) * entries
    return jnp.clip(entries, min=-limit, max=limit).astype(held_as)


def bell_draw_with(own_key, shape, deviation, limit, cuts, heavy, kind=jnp.bfloat16):
    values = deviation * jax.random.normal(own_key, shape, jnp.float32)
    if cuts:
        values = values * levels(own_key, shape, cuts, -0.22, 0.18)
    return jnp.clip(strengthened(values, jax.random.fold_in(own_key, 3), *heavy), -limit, limit).astype(kind)


def setup_inputs(seed: int = 0) -> dict:
    key_list = jax.random.split(jax.random.key(seed), 20)
    tokens = gaussian(key_list[0], (MICRO, ROWS, SEQ, D), 1.0, 6.0, ((1, 64),))
    pixels = gaussian(key_list[1], (MICRO, ROWS, VARS, PIX, SEQ), 1.0, 6.0, ((1, 64),))
    segments = jax.vmap(lambda own: jnp.searchsorted(jnp.cumsum(ragged(own, SEGS, SEQ, SEQ // 2, 1)), jnp.arange(SEQ), side="right"))(jax.random.split(key_list[2], MICRO * ROWS)).reshape((MICRO, ROWS, SEQ)).astype(jnp.int32)
    embed_weight = gaussian(key_list[3], (LAYERS, VARS, PIX, D), PIX ** -0.5, 3.0, ((0, 2),))
    var_embed = gaussian(key_list[4], (LAYERS, VARS, D), 1.0, 6.0, ((0, 2),))
    var_query = gaussian(key_list[5], (LAYERS, D), 1.0, 6.0, ((0, 2),))
    query_weight = gaussian(key_list[6], (LAYERS, D, D), D ** -0.5, 0.1875, ((0, 2),))
    key_weight = gaussian(key_list[7], (LAYERS, D, D), D ** -0.5, 0.1875, ((0, 2),))
    value_weight = gaussian(key_list[8], (LAYERS, D, D), D ** -0.5, 0.1875, ((0, 2),))
    pool_weight = gaussian(key_list[9], (LAYERS, D, D), (D // 4) ** -0.5, 0.375, ((0, 2),))
    first_gain = jnp.clip(1.0 + 0.1 * jax.random.normal(key_list[10], (LAYERS, D), jnp.float32), 0.5, 1.5).astype(jnp.bfloat16)
    project_in = gaussian(key_list[11], (LAYERS, D, 3 * D), D ** -0.5, 0.1875, ((0, 2),))
    project_out = gaussian(key_list[12], (LAYERS, D, D), (D // 8) ** -0.5, 0.5, ((0, 2),))
    second_gain = jnp.clip(1.0 + 0.1 * jax.random.normal(key_list[13], (LAYERS, D), jnp.float32), 0.5, 1.5).astype(jnp.bfloat16)
    up_weight = gaussian(key_list[14], (LAYERS, D, FF), D ** -0.5, 0.1875, ((0, 2),))
    up_bias = gaussian(key_list[15], (LAYERS, FF), 0.5, 3.0, ((0, 2),))
    down_weight = gaussian(key_list[16], (LAYERS, FF, D), FF ** -0.5, 0.09375, ((0, 2),))
    down_bias = gaussian(key_list[17], (LAYERS, D), 0.5, 3.0, ((0, 2),))
    cotangent = bell_draw_with(key_list[18], (MICRO, ROWS, SEQ, D), 1.0, 16.0, ((1, 64),), (1, 3, 64, 4.0))
    return dict(tokens=tokens, pixels=pixels, segments=segments, embed_weight=embed_weight, var_embed=var_embed, var_query=var_query, query_weight=query_weight, key_weight=key_weight, value_weight=value_weight, pool_weight=pool_weight, first_gain=first_gain, project_in=project_in, project_out=project_out, second_gain=second_gain, up_weight=up_weight, up_bias=up_bias, down_weight=down_weight, down_bias=down_bias, cotangent=cotangent)


@jax.custom_vjp
def low(v):
    return lax.optimization_barrier(v.astype(jnp.bfloat16)).astype(jnp.float32)

@jax.custom_vjp
def low_back(v):
    return v

def low_keep(v):
    return (low(v), None)

def low_pass(kept, grad):
    return (grad,)

def back_keep(v):
    return (v, None)

def back_low(kept, grad):
    return (low(grad),)
low.defvjp(low_keep, low_pass)
low_back.defvjp(back_keep, back_low)
MASK_FILL = -1000000000.0
NORM_EPS = 1e-06

def normalize(value):
    center = value - lax.optimization_barrier(jnp.mean(value, axis=-1, keepdims=True))
    return center * lax.rsqrt(lax.optimization_barrier(jnp.mean(center * center, axis=-1, keepdims=True)) + NORM_EPS)

def layer(inputs, patch_px, seg_ids, params):
    embed_w, var_emb, var_q, query_w, key_w, value_w, pool_w, gain_one, proj_in, proj_out, gain_two, up_w, up_b, down_w, down_b = params
    highest = lax.Precision.HIGHEST
    seq_len = inputs.shape[0]
    embedded = low_back(low(jnp.einsum('vps,vpd->svd', patch_px, embed_w, precision=highest) + var_emb[None]))
    query_vec = low(jnp.dot(var_q, query_w, precision=highest))
    probe = low(jnp.einsum('dhj,hj->hd', key_w.reshape(D, HEADS, HEAD), query_vec.reshape(HEADS, HEAD), precision=highest))
    var_scores = low_back(jnp.einsum('svd,hd->shv', embedded, probe, precision=highest) * 0.125)
    var_weights = low(jax.nn.softmax(var_scores, axis=-1))
    pooled = low_back(low(jnp.einsum('shv,svd->shd', var_weights, embedded, precision=highest)))
    mixed_vars = low_back(low(jnp.einsum('shd,dhj->shj', pooled, value_w.reshape(D, HEADS, HEAD), precision=highest).reshape(seq_len, D)))
    stream = inputs + low_back(jnp.dot(mixed_vars, pool_w, precision=highest))
    attn_in = low(normalize(stream) * gain_one)
    qkv = jnp.dot(attn_in, proj_in, precision=highest)
    queries = low_back(low(qkv[:, :D])).reshape(seq_len, HEADS, HEAD)
    keys = low_back(low(qkv[:, D:2 * D])).reshape(seq_len, HEADS, HEAD)
    values = low_back(low(qkv[:, 2 * D:])).reshape(seq_len, HEADS, HEAD)
    same = seg_ids[:, None] == seg_ids[None, :]
    raw = jnp.einsum('shj,thj->hst', queries, keys, precision=highest) * 0.125
    scores = low_back(jnp.where(same[None], raw, MASK_FILL))
    prob = low(jax.nn.softmax(scores, axis=-1))
    attended = low_back(low(jnp.einsum('hst,thj->shj', prob, values, precision=highest).reshape(seq_len, D)))
    stream_two = stream + low_back(jnp.dot(attended, proj_out, precision=highest))
    mlp_in = low(normalize(stream_two) * gain_two)
    pre_act = low_back(jnp.dot(mlp_in, up_w, precision=highest) + up_b)
    hidden = low_back(low(jax.nn.gelu(pre_act, approximate=False)))
    return stream_two + low_back(jnp.dot(hidden, down_w, precision=highest) + down_b)

def two_layers(tok_group, zero_group, px_group, seg_group, first_params, second_params):
    out_one = jax.vmap(lambda a, b, c: layer(a, b, c, first_params))(tok_group, px_group, seg_group)
    passed = low_back(low(out_one)) + zero_group
    out_two = jax.vmap(lambda a, b, c: layer(a, b, c, second_params))(passed, px_group, seg_group)
    return (out_one, out_two)

def reference(tokens, pixels, segments, embed_weight, var_embed, var_query, query_weight, key_weight, value_weight, pool_weight, first_gain, project_in, project_out, second_gain, up_weight, up_bias, down_weight, down_bias, cotangent):
    stacked = (embed_weight, var_embed, var_query, query_weight, key_weight, value_weight, pool_weight, first_gain, project_in, project_out, second_gain, up_weight, up_bias, down_weight, down_bias)
    first_params = tuple((w[0].astype(jnp.float32) for w in stacked))
    second_params = tuple((w[1].astype(jnp.float32) for w in stacked))
    num_seq = MICRO * ROWS
    group = math.gcd(num_seq, max(1, 1024 // SEQ))
    groups = num_seq // group
    tok_all = tokens.astype(jnp.float32).reshape(groups, group, SEQ, D)
    px_all = pixels.astype(jnp.float32).reshape(groups, group, VARS, PIX, SEQ)
    seg_all = segments.reshape(groups, group, SEQ)
    cot_all = cotangent.astype(jnp.float32).reshape(groups, group, SEQ, D)

    def step(carry, pieces):
        tok_group, px_group, seg_group, cot_group = pieces
        zero_group = jnp.zeros_like(tok_group)
        outs, pull = jax.vjp(lambda a, z, f, s: two_layers(a, z, px_group, seg_group, f, s), tok_group, zero_group, first_params, second_params)
        grad_tok, grad_pass, grad_first, grad_second = pull((jnp.zeros_like(outs[0]), cot_group))
        carry = (jax.tree.map(jnp.add, carry[0], grad_first), jax.tree.map(jnp.add, carry[1], grad_second))
        return (carry, (outs[0].astype(jnp.bfloat16), outs[1].astype(jnp.bfloat16), grad_tok, grad_pass))
    init = (jax.tree.map(jnp.zeros_like, first_params), jax.tree.map(jnp.zeros_like, second_params))
    totals, (out_one, out_two, grad_tok, grad_pass) = lax.scan(step, init, (tok_all, px_all, seg_all, cot_all))
    shape_out = (MICRO, ROWS, SEQ, D)
    layer_outputs = jnp.stack([out_one.reshape(shape_out), out_two.reshape(shape_out)])
    input_grads = jnp.stack([grad_tok.reshape(shape_out), grad_pass.reshape(shape_out)])
    grads = tuple((jnp.stack([first, second]) for first, second in zip(totals[0], totals[1])))
    return (layer_outputs, input_grads, grads[0], grads[1], grads[2], grads[3], grads[4], grads[5], grads[6], grads[7], grads[8], grads[9], grads[10], grads[11], grads[12], grads[13], grads[14])
```

```python
from functools import partial

import jax
import jax.numpy as jnp
from jax import lax
from jax.sharding import PartitionSpec as P

HEADS = 16
HEAD = 64
VARS = 48
PIX = 4
SIDE = 4
MASK_FILL = -1000000000.0
NORM_EPS = 1e-06
STRIDE = {"x": 1, "y": SIDE, "z": SIDE * SIDE}
BF = jnp.bfloat16
F32 = jnp.float32


def dot(a, b, contract):
    return lax.dot_general(a, b, (contract, ((), ())), preferred_element_type=F32)


def moved(axis, step):
    chips = SIDE**3
    pairs = []
    for section in (0, 1):
        signed = step if section == 0 else -step
        for chip in range(chips):
            at = (chip // STRIDE[axis]) % SIDE
            to = chip + ((at + signed) % SIDE - at) * STRIDE[axis]
            pairs.append((section * chips + chip, section * chips + to))
    return pairs


def swap(value, axis, step):
    return lax.ppermute(value, ("section", "batch"), moved(axis, step))


def place(axis):
    return (lax.axis_index("batch") // STRIDE[axis]) % SIDE


def other(axis, step):
    sign = jnp.where(lax.axis_index("section") == 0, 1, -1)
    return (place(axis) + sign * step) % SIDE


def picked(value, index, dim):
    return lax.dynamic_index_in_dim(value, index, dim, keepdims=False)


def share(value, axis):
    return [value] + [swap(value, axis, k) for k in (1, 2, 3)]


def deal(value, axis, dim):
    mine = picked(value, place(axis), dim)
    return [mine] + [swap(picked(value, other(axis, k), dim), axis, k) for k in (1, 2, 3)]


def added(parts):
    total = parts[0].astype(F32)
    for part in parts[1:]:
        total = total + part.astype(F32)
    return total


def set_back(parts, axis, dim):
    shape = list(parts[0].shape)
    shape.insert(dim, SIDE)
    out = jnp.zeros(shape, parts[0].dtype)
    out = lax.dynamic_update_index_in_dim(out, parts[0], place(axis), dim)
    for k in (1, 2, 3):
        out = lax.dynamic_update_index_in_dim(out, parts[k], other(axis, -k), dim)
    return out


def normalize(value):
    center = value - jnp.mean(value, axis=-1, keepdims=True)
    factor = lax.rsqrt(jnp.mean(center * center, axis=-1, keepdims=True) + NORM_EPS)
    return (center * factor, factor)


def norm_back(grad, normed, factor):
    return factor * (
        grad
        - jnp.mean(grad, axis=-1, keepdims=True)
        - normed * jnp.mean(grad * normed, axis=-1, keepdims=True)
    )


def prepare(embed_w, var_emb, var_q, query_w, key_w, value_w):
    width = query_w.shape[0]
    table = jnp.concatenate([embed_w.transpose(1, 0, 2).reshape(PIX * VARS, width), var_emb])
    query_vec = dot(var_q[None], query_w, ((1,), (0,)))[0].astype(BF)
    probe = jnp.einsum(
        "dhj,hj->hd",
        key_w.reshape(width, HEADS, HEAD),
        query_vec.reshape(HEADS, HEAD),
        preferred_element_type=F32,
    ).astype(BF)
    quick = dot(table, probe, ((1,), (1,))) * 0.125
    value_table = dot(table, value_w, ((1,), (0,))).astype(BF)
    return table, query_vec, probe, quick, value_table


def attention_scores(qkv, seg_ids, width):
    tokens = qkv.shape[0]
    queries = qkv[:, :width].reshape(tokens, HEADS, HEAD)
    keys = qkv[:, width : 2 * width].reshape(tokens, HEADS, HEAD)
    values = qkv[:, 2 * width :].reshape(tokens, HEADS, HEAD)
    same = seg_ids[:, None] == seg_ids[None, :]
    raw = jnp.einsum("shj,thj->hst", queries, keys, preferred_element_type=F32) * 0.125
    return (jnp.where(same[None], raw, MASK_FILL), queries, keys, values)


def forward(inputs, patch, seg_ids, quick, value_table, weights):
    pool_w, gain_one, proj_in, proj_out, gain_two, up_w, up_b, down_w, down_b = weights
    tokens, width = inputs.shape
    var_scores = jnp.einsum("pvh,pvt->hvt", quick.reshape(PIX + 1, VARS, HEADS), patch.astype(F32), precision=lax.Precision.HIGHEST)
    var_prob = jax.nn.softmax(var_scores, axis=1)
    blend = (var_prob[:, None] * patch[None].astype(F32)).astype(BF)
    blend = blend.reshape(HEADS, (PIX + 1) * VARS, tokens)
    mixed = jnp.einsum(
        "khj,hkt->hjt", value_table.reshape(-1, HEADS, HEAD), blend, preferred_element_type=F32
    )
    mixed = mixed.astype(BF).reshape(width, tokens)
    stream = inputs.astype(F32) + dot(mixed, pool_w, ((0,), (0,)))
    normed_one, factor_one = normalize(stream)
    attn_in = (normed_one * gain_one.astype(F32)).astype(BF)
    qkv = dot(attn_in, proj_in, ((1,), (0,))).astype(BF)
    scores, queries, keys, values = attention_scores(qkv, seg_ids, width)
    top = jnp.max(scores, axis=-1, keepdims=True)
    log_total = top + jnp.log(jnp.sum(jnp.exp(scores - top), axis=-1, keepdims=True))
    prob = jnp.exp(scores - log_total)
    attended = (
        jnp.einsum("hst,thj->shj", prob.astype(BF), values, preferred_element_type=F32)
        .astype(BF)
        .reshape(tokens, width)
    )
    stream_two = stream + dot(attended, proj_out, ((1,), (0,)))
    normed_two, factor_two = normalize(stream_two)
    mlp_in = (normed_two * gain_two.astype(F32)).astype(BF)
    pre_act = dot(mlp_in, up_w, ((1,), (0,))) + up_b.astype(F32)
    hidden = jax.nn.gelu(pre_act, approximate=False).astype(BF)
    result = stream_two + dot(hidden, down_w, ((1,), (0,))) + down_b.astype(F32)
    saved = (
        var_prob,
        blend,
        mixed,
        normed_one,
        factor_one,
        attn_in,
        qkv,
        log_total,
        attended,
        normed_two,
        factor_two,
        mlp_in,
        pre_act,
        hidden,
    )
    return (result.astype(BF), saved)


def backward(grad_out, saved, patch, seg_ids, value_table, weights):
    pool_w, gain_one, proj_in, proj_out, gain_two, up_w, up_b, down_w, down_b = weights
    (
        var_prob,
        blend,
        mixed,
        normed_one,
        factor_one,
        attn_in,
        qkv,
        log_total,
        attended,
        normed_two,
        factor_two,
        mlp_in,
        pre_act,
        hidden,
    ) = saved
    tokens, width = grad_out.shape
    branch_down = grad_out
    grad_down_b = jnp.sum(branch_down.astype(F32), axis=0)
    grad_hidden = dot(branch_down, down_w, ((1,), (1,))).astype(BF)
    gelu_out, gelu_pull = jax.vjp(partial(jax.nn.gelu, approximate=False), pre_act)
    grad_pre = gelu_pull(grad_hidden.astype(F32))[0].astype(BF)
    grad_up_b = jnp.sum(grad_pre.astype(F32), axis=0)
    grad_mlp_in = dot(grad_pre, up_w, ((1,), (1,)))
    grad_gain_two = jnp.sum(grad_mlp_in * normed_two, axis=0)
    grad_stream_two = grad_out.astype(F32) + norm_back(
        grad_mlp_in * gain_two.astype(F32), normed_two, factor_two
    )
    branch_proj = grad_stream_two.astype(BF)
    grad_attended = dot(branch_proj, proj_out, ((1,), (1,))).astype(BF).reshape(tokens, HEADS, HEAD)
    scores, queries, keys, values = attention_scores(qkv, seg_ids, width)
    prob = jnp.exp(scores - log_total)
    grad_prob = jnp.einsum("shj,thj->hst", grad_attended, values, preferred_element_type=F32)
    grad_values = jnp.einsum(
        "hst,shj->thj", prob.astype(BF), grad_attended, preferred_element_type=F32
    )
    grad_scores = (prob * (grad_prob - jnp.sum(grad_prob * prob, axis=-1, keepdims=True))).astype(BF)
    grad_queries = jnp.einsum("hst,thj->shj", grad_scores, keys, preferred_element_type=F32) * 0.125
    grad_keys = jnp.einsum("hst,shj->thj", grad_scores, queries, preferred_element_type=F32) * 0.125
    grad_qkv = jnp.concatenate(
        [
            grad_queries.reshape(tokens, width),
            grad_keys.reshape(tokens, width),
            grad_values.reshape(tokens, width),
        ],
        axis=1,
    ).astype(BF)
    grad_attn_in = dot(grad_qkv, proj_in, ((1,), (1,)))
    grad_gain_one = jnp.sum(grad_attn_in * normed_one, axis=0)
    grad_stream = grad_stream_two + norm_back(
        grad_attn_in * gain_one.astype(F32), normed_one, factor_one
    )
    branch_pool = grad_stream.astype(BF)
    grad_mixed = dot(branch_pool, pool_w, ((1,), (1,))).astype(BF).reshape(tokens, HEADS, HEAD)
    grad_blend = jnp.einsum(
        "khj,thj->hkt",
        value_table.reshape(-1, HEADS, HEAD),
        grad_mixed,
        preferred_element_type=F32,
    ).reshape(HEADS, PIX + 1, VARS, tokens)
    grad_var_prob = jnp.sum(grad_blend * patch[None].astype(F32), axis=1)
    grad_var_scores = var_prob * (
        grad_var_prob - jnp.sum(grad_var_prob * var_prob, axis=1, keepdims=True)
    )
    value_term = jnp.einsum("hkt,thj->hjk", blend, grad_mixed, preferred_element_type=F32)
    value_term = value_term.reshape(width, (PIX + 1) * VARS)
    score_term = (
        jnp.einsum("pvt,hvt->pvh", patch, grad_var_scores.astype(BF), preferred_element_type=F32)
        * 0.125
    ).reshape((PIX + 1) * VARS, HEADS)
    lines = jnp.concatenate(
        [grad_down_b, grad_gain_two, grad_gain_one, grad_up_b]
    )
    return (
        grad_stream,
        grad_pre,
        branch_proj,
        grad_qkv,
        branch_pool,
        value_term.astype(BF),
        score_term,
        lines,
    )


def quarters(value):
    tokens, columns = value.shape
    return value.reshape(tokens, SIDE, columns // SIDE)


def joined(parts):
    return jnp.concatenate(parts, axis=0)


def local(
    tokens,
    pixels,
    segments,
    embed_weight,
    var_embed,
    var_query,
    query_weight,
    key_weight,
    value_weight,
    pool_weight,
    first_gain,
    project_in,
    project_out,
    second_gain,
    up_weight,
    up_bias,
    down_weight,
    down_bias,
    cotangent,
):
    is_first = lax.axis_index("section") == 0
    micro, _, seq, width = tokens.shape
    rows = micro * seq
    value_w, query_w, key_w, var_q = value_weight[0], query_weight[0], key_weight[0], var_query[0]
    weights = tuple(
        w[0]
        for w in (
            pool_weight,
            first_gain,
            project_in,
            project_out,
            second_gain,
            up_weight,
            up_bias,
            down_weight,
            down_bias,
        )
    )
    table, query_vec, probe, quick, value_table = prepare(
        embed_weight[0], var_embed[0], var_q, query_w, key_w, value_w
    )
    patch = pixels[:, 0].transpose(2, 1, 0, 3).reshape(PIX, VARS, rows)
    patch = jnp.concatenate([patch, jnp.ones((1, VARS, rows), BF)])
    seg_ids = (segments[:, 0] + SIDE * jnp.arange(micro)[:, None]).reshape(rows)
    inputs = tokens.reshape(rows, width)

    first = forward(inputs, patch, seg_ids, quick, value_table, weights)
    passed = lax.ppermute(first[0], "section", [(0, 1)])
    result, saved = lax.cond(
        is_first,
        lambda: first,
        lambda: forward(passed, patch, seg_ids, quick, value_table, weights),
    )
    mixed, attn_in, attended, mlp_in, hidden = saved[2], saved[5], saved[8], saved[11], saved[13]

    mlp_in_all = joined(share(mlp_in, "x"))
    mixed_all = jnp.concatenate(share(mixed, "x"), axis=1)
    hidden_all = joined(deal(quarters(hidden), "y", 1))
    attended_all = joined(share(attended, "y"))
    attn_in_all = joined(share(attn_in, "z"))

    top_grad = cotangent.reshape(rows, width)
    second = backward(top_grad, saved, patch, seg_ids, value_table, weights)
    passed = lax.ppermute(second[0].astype(BF), "section", [(1, 0)])
    branch_down = jnp.where(is_first, passed, top_grad)
    back = lax.cond(
        is_first,
        lambda: backward(passed, saved, patch, seg_ids, value_table, weights),
        lambda: second,
    )
    grad_in, grad_pre, branch_proj, grad_qkv, branch_pool, value_term, score_term, lines = back

    branch_down_all = joined(share(branch_down, "y"))
    grad_pre_all = joined(deal(quarters(grad_pre), "x", 1))
    branch_proj_all = joined(deal(quarters(branch_proj), "y", 1))
    grad_qkv_all = joined(deal(quarters(grad_qkv), "z", 1))
    branch_pool_all = joined(deal(quarters(branch_pool), "x", 1))

    up_term = dot(mlp_in_all, grad_pre_all, ((0,), (0,))).astype(BF)
    down_term = dot(branch_down_all, hidden_all, ((0,), (0,))).astype(BF)
    in_term = dot(attn_in_all, grad_qkv_all, ((0,), (0,))).astype(BF)
    out_term = dot(attended_all, branch_proj_all, ((0,), (0,))).astype(BF)
    pool_term = dot(mixed_all, branch_pool_all, ((1,), (0,))).astype(BF)

    def cube(value):
        return value.reshape(SIDE, SIDE, SIDE, -1, value.shape[-1])

    along_x = jnp.concatenate([up_term, pool_term], axis=1)
    along_y = jnp.concatenate([down_term, out_term], axis=1)
    along_z = in_term
    along_x = added(deal(cube(along_x), "y", 1)).astype(BF)
    along_y = added(deal(cube(along_y), "z", 0)).astype(BF)
    along_z = added(deal(cube(along_z), "x", 2)).astype(BF)
    along_x = added(deal(along_x, "z", 0)).astype(BF)
    along_y = added(deal(along_y, "x", 1)).astype(BF)
    along_z = added(deal(along_z, "y", 1)).astype(BF)
    along_x = set_back(deal(along_x, "x", 0), "x", 1).astype(F32)
    along_y = set_back(deal(along_y, "y", 0), "y", 1).astype(F32)
    along_z = set_back(deal(along_z, "z", 0), "z", 1).astype(F32)
    own = along_x.shape[0]
    wide = up_term.shape[1]
    grad_up = along_x[..., :wide].reshape(own, -1)
    grad_pool = along_x[..., wide:].reshape(own, -1)
    grad_down = along_y[..., :wide].reshape(own, -1).T
    grad_out = along_y[..., wide:].reshape(own, -1)
    grad_in_w = along_z.reshape(own, -1)

    value_sum = cube(value_term)
    for axis, dim in (("x", 2), ("y", 1), ("z", 0)):
        value_sum = added(deal(value_sum, axis, dim)).astype(BF)
    for axis, dim in (("z", 0), ("y", 1), ("x", 2)):
        value_sum = set_back(share(value_sum, axis), axis, dim)
    value_sum = value_sum.reshape(width, -1)
    small = jnp.concatenate([score_term.reshape(-1), lines])
    for axis in ("x", "y", "z"):
        small = added(share(small, axis))
    score_sum = small[: score_term.size].reshape(score_term.shape)
    lines = small[score_term.size :]
    at = lax.axis_index("batch") * own
    mine = partial(lax.dynamic_slice_in_dim, start_index=at, slice_size=own)
    precise = partial(jnp.einsum, precision=lax.Precision.HIGHEST, preferred_element_type=F32)
    table_mine = mine(table, axis=1)
    grad_value = dot(table_mine, value_sum, ((0,), (1,)))
    grad_table = dot(value_sum, mine(value_w, axis=0), ((0,), (1,)))
    grad_table = grad_table + precise("kh,hd->kd", score_sum, mine(probe, axis=1).astype(F32))
    grad_probe = precise("kh,kd->hd", score_sum, table.astype(F32))
    grad_qvec = jnp.einsum(
        "hd,dhj->hj", grad_probe, key_w.reshape(width, HEADS, HEAD).astype(F32)
    ).reshape(width)
    grad_key = (
        mine(grad_probe, axis=1).T[:, :, None] * query_vec.astype(F32).reshape(1, HEADS, HEAD)
    ).reshape(own, width)
    grad_qw = mine(var_q, axis=0).astype(F32)[:, None] * grad_qvec[None]
    grad_vq = jnp.dot(mine(query_w, axis=0).astype(F32), grad_qvec)
    grad_embed = grad_table[: PIX * VARS].reshape(PIX, VARS, own).transpose(1, 0, 2)
    grad_var = grad_table[PIX * VARS :]
    line_down = mine(lines[:width], axis=0)
    line_two = mine(lines[width : 2 * width], axis=0)
    line_one = mine(lines[2 * width : 3 * width], axis=0)
    line_up = lax.dynamic_slice_in_dim(lines[3 * width :], at * SIDE, own * SIDE)

    return (
        result.reshape(1, micro, 1, seq, width),
        grad_in.reshape(1, micro, 1, seq, width),
        grad_embed[None],
        grad_var[None],
        grad_vq[None],
        grad_qw[None],
        grad_key[None],
        grad_value[None],
        grad_pool[None],
        line_one[None],
        grad_in_w[None],
        grad_out[None],
        line_two[None],
        grad_up[None],
        line_up[None],
        grad_down[None],
        line_down[None],
    )


def solution(mesh):
    in_specs = (
        P(None, "batch", None, None),
        P(None, "batch", None, None, None),
        P(None, "batch", None),
        P("section", None, None, None),
        P("section", None, None),
        P("section", None),
        P("section", None, None),
        P("section", None, None),
        P("section", None, None),
        P("section", None, None),
        P("section", None),
        P("section", None, None),
        P("section", None, None),
        P("section", None),
        P("section", None, None),
        P("section", None),
        P("section", None, None),
        P("section", None),
        P(None, "batch", None, None),
    )
    out_specs = (
        P("section", None, "batch", None, None),
        P("section", None, "batch", None, None),
        P("section", None, None, "batch"),
        P("section", None, "batch"),
        P("section", "batch"),
        P("section", "batch", None),
        P("section", "batch", None),
        P("section", "batch", None),
        P("section", "batch", None),
        P("section", "batch"),
        P("section", "batch", None),
        P("section", "batch", None),
        P("section", "batch"),
        P("section", "batch", None),
        P("section", "batch"),
        P("section", None, "batch"),
        P("section", "batch"),
    )
    return jax.shard_map(local, mesh=mesh, in_specs=in_specs, out_specs=out_specs, check_vma=False)
```

```python
from functools import partial

import jax
import jax.numpy as jnp
from jax import lax
from jax.experimental import pallas as pl
from jax.experimental.pallas import tpu as pltpu
from jax.sharding import PartitionSpec as P

HEADS = 16
HEAD = 64
VARS = 48
PIX = 4
SIDE = 4
MASK_FILL = -1000000000.0
NORM_EPS = 1e-06
STRIDE = {"x": 1, "y": SIDE, "z": SIDE * SIDE}
BF = jnp.bfloat16
F32 = jnp.float32


def dot(a, b, contract):
    return lax.dot_general(a, b, (contract, ((), ())), preferred_element_type=F32)


def moved(axis, step):
    chips = SIDE**3
    pairs = []
    for section in (0, 1):
        signed = step if section == 0 else -step
        for chip in range(chips):
            at = (chip // STRIDE[axis]) % SIDE
            to = chip + ((at + signed) % SIDE - at) * STRIDE[axis]
            pairs.append((section * chips + chip, section * chips + to))
    return pairs


def swap(value, axis, step):
    return lax.ppermute(value, ("section", "batch"), moved(axis, step))


def place(axis):
    return (lax.axis_index("batch") // STRIDE[axis]) % SIDE


def other(axis, step):
    sign = jnp.where(lax.axis_index("section") == 0, 1, -1)
    return (place(axis) + sign * step) % SIDE


def picked(value, index, dim):
    return lax.dynamic_index_in_dim(value, index, dim, keepdims=False)


def share(value, axis):
    return [value] + [swap(value, axis, k) for k in (1, 2, 3)]


def deal(value, axis, dim):
    mine = picked(value, place(axis), dim)
    return [mine] + [swap(picked(value, other(axis, k), dim), axis, k) for k in (1, 2, 3)]


def added(parts):
    total = parts[0].astype(F32)
    for part in parts[1:]:
        total = total + part.astype(F32)
    return total


def set_back(parts, axis, dim):
    shape = list(parts[0].shape)
    shape.insert(dim, SIDE)
    out = jnp.zeros(shape, parts[0].dtype)
    out = lax.dynamic_update_index_in_dim(out, parts[0], place(axis), dim)
    for k in (1, 2, 3):
        out = lax.dynamic_update_index_in_dim(out, parts[k], other(axis, -k), dim)
    return out


VM = pl.BlockSpec(memory_space=pltpu.VMEM)
SM = pl.BlockSpec(memory_space=pltpu.SMEM)
HB = pl.BlockSpec(memory_space=pl.ANY)
BIG = 60 * 1024 * 1024
ROWS = 256
WIDTH = HEADS * HEAD
FF = 4096
TILE = 512
KEYS = (PIX + 1) * VARS
PAIR = 2 * HEAD
PAIRS = HEADS // 2
NN = ((1,), (0,))
NT = ((1,), (1,))
TN = ((0,), (0,))


def span(index, size):
    return pl.ds(pl.multiple_of(index * size, size), size)


def shape(dims, dtype):
    return jax.ShapeDtypeStruct(dims, dtype)


def prepare_kernel(table, var_q, query_w, key_w, value_w, query_vec, probe, quick, value_t):
    found = dot(jnp.broadcast_to(var_q[...], (16, WIDTH)), query_w[...], NN).astype(BF)
    query_vec[...] = found[0:1].astype(F32)
    head = lax.broadcasted_iota(jnp.int32, (16, WIDTH), 0)
    lane = lax.broadcasted_iota(jnp.int32, (16, WIDTH), 1)
    spread = jnp.where(lane // HEAD == head, found.astype(F32), 0.0).astype(BF)
    made = dot(spread, key_w[...], NT).astype(BF)
    probe[...] = made.astype(F32)
    quick[...] = dot(table[...], made, NT) * 0.125
    value_t[...] = dot(table[...], value_w[...], NN).T.astype(BF)


def prepare(table, var_q, query_w, key_w, value_w):
    return pl.pallas_call(
        prepare_kernel,
        out_shape=(
            shape((1, WIDTH), F32),
            shape((HEADS, WIDTH), F32),
            shape((KEYS, HEADS), F32),
            shape((WIDTH, KEYS), BF),
        ),
        in_specs=[VM] * 5,
        out_specs=(VM,) * 4,
        compiler_params=pltpu.CompilerParams(vmem_limit_bytes=BIG),
    )(table, var_q, query_w, key_w, value_w)


def normalize(value):
    center = value - jnp.mean(value, axis=-1, keepdims=True)
    factor = lax.rsqrt(jnp.mean(center * center, axis=-1, keepdims=True) + NORM_EPS)
    return (center * factor, factor)


def norm_back(grad, normed, factor):
    return factor * (
        grad
        - jnp.mean(grad, axis=-1, keepdims=True)
        - normed * jnp.mean(grad * normed, axis=-1, keepdims=True)
    )


def halves():
    lane = lax.broadcasted_iota(jnp.int32, (1, PAIR), 1)
    return [jnp.where(lane // HEAD == half, 1.0, 0.0).astype(BF) for half in (0, 1)]


def column(value, index):
    lane = lax.broadcasted_iota(jnp.int32, value.shape, 1)
    return jnp.sum(jnp.where(lane == index, value, 0.0), axis=-1, keepdims=True)


FORWARD_OUT = (
    shape((ROWS, WIDTH), BF),
    shape((HEADS, VARS, ROWS), F32),
    shape((ROWS, WIDTH), F32),
    shape((ROWS, WIDTH), F32),
    shape((ROWS, 3 * WIDTH), BF),
    shape((ROWS, 128), F32),
    shape((ROWS, FF), BF),
    shape((ROWS, 2 * WIDTH), BF),
    shape((SIDE, ROWS, FF // SIDE), BF),
    shape((ROWS, 2 * WIDTH), BF),
)


def forward_kernel(again, *refs):
    (active, inputs, patch, seg_c, seg_r, quick, value_t, gain_one, gain_two, up_b, down_b) = refs[:11]
    weights = refs[11:16]
    refs = refs[16:]
    n = len(FORWARD_OUT)
    if again:
        refs = refs[n:]
    outs, held = refs[:n], refs[n : 2 * n]
    pool_w, proj_in, proj_out, up_w, down_w = refs[2 * n : 2 * n + 5]
    blend, mask, acc, w_sem, o_sem = refs[2 * n + 5 :]
    result, prob_o, stream_o, two_o, qkv_o, lse_o, slope_o, for_x, for_y, for_z = held

    @pl.when(active[0] == 1)
    def _():
        def fetch(i):
            return pltpu.make_async_copy(
                weights[i], (pool_w, proj_in, proj_out, up_w, down_w)[i], w_sem.at[i]
            )

        def put(i):
            return pltpu.make_async_copy(held[i], outs[i], o_sem.at[i])

        for i in range(5):
            fetch(i).start()
        for pair in range(PAIRS):
            both = []
            for head in (2 * pair, 2 * pair + 1):
                score = quick[PIX * VARS :, head : head + 1] + jnp.zeros((VARS, ROWS), F32)
                for p in range(PIX):
                    score = score + quick[p * VARS : (p + 1) * VARS, head : head + 1] * patch[p]
                grown = jnp.exp(score - jnp.max(score, axis=0, keepdims=True))
                prob = grown / jnp.sum(grown, axis=0, keepdims=True)
                prob_o[head] = prob
                for p in range(PIX):
                    blend[p * VARS : (p + 1) * VARS] = (prob * patch[p]).astype(BF)
                blend[PIX * VARS :] = prob.astype(BF)
                both.append(dot(value_t[head * HEAD : (head + 1) * HEAD], blend[...], NN))
            at = WIDTH + pair * PAIR
            for_z[:, at : at + PAIR] = jnp.concatenate(both, axis=0).T.astype(BF)
        put(1).start()
        fetch(0).wait()
        stream = inputs[...].astype(F32) + dot(for_z[:, WIDTH:], pool_w[...], NN)
        stream_o[...] = stream
        put(2).start()
        normed, _ = normalize(stream)
        for_z[:, :WIDTH] = (normed * gain_one[...].astype(F32)).astype(BF)
        put(9).start()
        fetch(1).wait()

        def project(i, c):
            qkv_o[:, span(i, TILE)] = dot(for_z[:, :WIDTH], proj_in[:, span(i, TILE)], NN).astype(BF)
            return c

        lax.fori_loop(0, 3 * WIDTH // TILE, project, 0)
        put(4).start()
        mask[...] = jnp.where(seg_c[...] == seg_r[...], 1.0, 0.0)
        halfs = halves()
        lane = lax.broadcasted_iota(jnp.int32, (ROWS, 128), 1)

        def attend(i, lse):
            q = qkv_o[:, span(i, PAIR)]
            k = qkv_o[:, span(PAIRS + i, PAIR)]
            v = qkv_o[:, span(2 * PAIRS + i, PAIR)]
            got = []
            for half in (0, 1):
                raw = dot(q * halfs[half], k, NT) * 0.125
                score = jnp.where(mask[...] > 0.5, raw, MASK_FILL)
                top = jnp.max(score, axis=-1, keepdims=True)
                grown = jnp.exp(score - top)
                total = jnp.sum(grown, axis=-1, keepdims=True)
                lse = jnp.where(lane == 2 * i + half, top + jnp.log(total), lse)
                got.append(dot((grown / total).astype(BF), v, NN))
            for_x[:, span(PAIRS + i, PAIR)] = jnp.where(lane < HEAD, got[0], got[1]).astype(BF)
            return lse

        lse_o[...] = lax.fori_loop(0, PAIRS, attend, jnp.zeros((ROWS, 128), F32))
        put(5).start()
        fetch(2).wait()
        two = stream_o[...] + dot(for_x[:, WIDTH:], proj_out[...], NN)
        two_o[...] = two
        put(3).start()
        normed, _ = normalize(two)
        for_x[:, :WIDTH] = (normed * gain_two[...].astype(F32)).astype(BF)
        put(7).start()
        acc[...] = two + down_b[...].astype(F32)
        fetch(3).wait()
        fetch(4).wait()

        def mlp(i, c):
            pre = dot(for_x[:, :WIDTH], up_w[:, span(i, TILE)], NN) + up_b[:, span(i, TILE)].astype(F32)
            cdf = 0.5 * (1.0 + lax.erf(pre * 0.7071067811865476))
            slope_o[:, span(i, TILE)] = (
                cdf + pre * (jnp.exp(-0.5 * pre * pre) * 0.3989422804014327)
            ).astype(BF)
            hid = (pre * cdf).astype(BF)
            per = FF // SIDE // TILE
            for_y[i // per, :, span(i % per, TILE)] = hid
            acc[...] += dot(hid, down_w[span(i, TILE), :], NN)
            return c

        lax.fori_loop(0, FF // TILE, mlp, 0)
        result[...] = acc[...].astype(BF)
        for i in (0, 6, 8):
            put(i).start()
        for i in range(n):
            put(i).wait()


def forward(active, inputs, base, lines, weights, earlier):
    again = earlier is not None
    given = (active, inputs, *base, *lines, *weights)
    return pl.pallas_call(
        partial(forward_kernel, again),
        out_shape=FORWARD_OUT,
        in_specs=[SM] + [VM] * 10 + [HB] * 5 + ([HB] * len(FORWARD_OUT) if again else []),
        out_specs=(HB,) * len(FORWARD_OUT),
        scratch_shapes=[pltpu.VMEM(o.shape, o.dtype) for o in FORWARD_OUT]
        + [pltpu.VMEM(w.shape, w.dtype) for w in weights]
        + [
            pltpu.VMEM((KEYS, ROWS), BF),
            pltpu.VMEM((ROWS, ROWS), F32),
            pltpu.VMEM((ROWS, WIDTH), F32),
            pltpu.SemaphoreType.DMA((5,)),
            pltpu.SemaphoreType.DMA((len(FORWARD_OUT),)),
        ],
        input_output_aliases={len(given) + i: i for i in range(len(FORWARD_OUT))} if again else {},
        compiler_params=pltpu.CompilerParams(vmem_limit_bytes=BIG),
        cost_estimate=pl.CostEstimate(flops=8 * 10**9, bytes_accessed=40 * 10**6, transcendentals=0),
    )(*given, *(earlier if again else ()))


MLP_OUT = (
    shape((SIDE, ROWS, (FF + WIDTH) // SIDE), BF),
    shape((ROWS, WIDTH), F32),
    shape((8, WIDTH), F32),
)


def mlp_back_kernel(again, *refs):
    active, grad, two, slope, gain_two, up_hbm, down_hbm = refs[:7]
    refs = refs[7:]
    n = len(MLP_OUT)
    if again:
        refs = refs[n:]
    outs, held = refs[:n], refs[n : 2 * n]
    up_w, down_w, acc, w_sem, o_sem = refs[2 * n :]
    pre_o, two_o, line_o = held

    @pl.when(active[0] == 1)
    def _():
        down_copy = pltpu.make_async_copy(down_hbm, down_w, w_sem.at[0])
        up_copy = pltpu.make_async_copy(up_hbm, up_w, w_sem.at[1])
        down_copy.start()
        up_copy.start()

        def put(i):
            return pltpu.make_async_copy(held[i], outs[i], o_sem.at[i])

        normed, factor = normalize(two[...])
        two_o[...] = normed
        acc[...] = jnp.zeros_like(acc)
        line_o[...] = jnp.zeros_like(line_o)
        down_copy.wait()
        up_copy.wait()
        per = FF // SIDE // TILE

        def mlp(i, c):
            hid = dot(grad[...], down_w[span(i, TILE), :], NT).astype(BF).astype(F32)
            pre = (hid * slope[:, span(i, TILE)].astype(F32)).astype(BF)
            pre_o[i // per, :, span(i % per, TILE)] = pre
            line_o[pl.ds(2 + i // per, 1), span(i % per, TILE)] = jnp.sum(
                pre.astype(F32), axis=0, keepdims=True
            )
            acc[...] += dot(pre, up_w[:, span(i, TILE)], NT)
            return c

        lax.fori_loop(0, FF // TILE, mlp, 0)
        normed = two_o[...]
        got = acc[...]
        line_o[0:1] = jnp.sum(got * normed, axis=0, keepdims=True)
        line_o[1:2] = jnp.sum(grad[...].astype(F32), axis=0, keepdims=True)
        back = grad[...].astype(F32) + norm_back(got * gain_two[...].astype(F32), normed, factor)
        two_o[...] = back
        for q in range(SIDE):
            part = WIDTH // SIDE
            pre_o[q, :, FF // SIDE :] = back[:, q * part : (q + 1) * part].astype(BF)
        for i in (0, 1, 2):
            put(i).start()
        for i in range(n):
            put(i).wait()


def mlp_back(active, grad, two, slope, gain_two, up_w, down_w, earlier):
    again = earlier is not None
    given = (active, grad, two, slope, gain_two, up_w, down_w)
    return pl.pallas_call(
        partial(mlp_back_kernel, again),
        out_shape=MLP_OUT,
        in_specs=[SM] + [VM] * 4 + [HB] * 2 + ([HB] * len(MLP_OUT) if again else []),
        out_specs=(HB,) * len(MLP_OUT),
        scratch_shapes=[pltpu.VMEM(o.shape, o.dtype) for o in MLP_OUT]
        + [
            pltpu.VMEM(up_w.shape, BF),
            pltpu.VMEM(down_w.shape, BF),
            pltpu.VMEM((ROWS, WIDTH), F32),
            pltpu.SemaphoreType.DMA((2,)),
            pltpu.SemaphoreType.DMA((len(MLP_OUT),)),
        ],
        input_output_aliases={len(given) + i: i for i in range(len(MLP_OUT))} if again else {},
        compiler_params=pltpu.CompilerParams(vmem_limit_bytes=BIG),
        cost_estimate=pl.CostEstimate(flops=5 * 10**9, bytes_accessed=25 * 10**6, transcendentals=0),
    )(*given, *(earlier if again else ()))


ATTEND_OUT = (
    shape((SIDE, ROWS, 3 * WIDTH // SIDE), BF),
    shape((ROWS, WIDTH), F32),
    shape((SIDE, ROWS, WIDTH // SIDE), BF),
    shape((8, WIDTH), F32),
)


def attend_back_kernel(again, *refs):
    active, grad_two, qkv, lse, seg_c, seg_r, stream, gain_one, in_hbm, out_hbm = refs[:10]
    refs = refs[10:]
    n = len(ATTEND_OUT)
    if again:
        refs = refs[n:]
    outs, held = refs[:n], refs[n : 2 * n]
    proj_in, proj_out, mask, given, w_sem, o_sem = refs[2 * n :]
    qkv_o, stream_o, pool_o, line_o = held

    @pl.when(active[0] == 1)
    def _():
        out_copy = pltpu.make_async_copy(out_hbm, proj_out, w_sem.at[0])
        in_copy = pltpu.make_async_copy(in_hbm, proj_in, w_sem.at[1])
        out_copy.start()
        in_copy.start()

        def put(i):
            return pltpu.make_async_copy(held[i], outs[i], o_sem.at[i])

        mask[...] = jnp.where(seg_c[...] == seg_r[...], 1.0, 0.0)
        halfs = halves()
        lane = lax.broadcasted_iota(jnp.int32, (ROWS, PAIR), 1)
        out_copy.wait()
        given[...] = dot(grad_two[...].astype(BF), proj_out[...], NT).astype(BF)
        per = 3 * WIDTH // SIDE // PAIR

        def attend(i, c):
            q = qkv[:, span(i, PAIR)]
            k = qkv[:, span(PAIRS + i, PAIR)]
            v = qkv[:, span(2 * PAIRS + i, PAIR)]
            g = given[:, span(i, PAIR)]
            dq, dk, dv = [], [], []
            for half in (0, 1):
                raw = dot(q * halfs[half], k, NT) * 0.125
                score = jnp.where(mask[...] > 0.5, raw, MASK_FILL)
                prob = jnp.exp(score - column(lse[...], 2 * i + half))
                grad_prob = dot(g * halfs[half], v, NT)
                inner = jnp.sum(grad_prob * prob, axis=-1, keepdims=True)
                grad_score = (prob * (grad_prob - inner)).astype(BF)
                dq.append(dot(grad_score, k, NN))
                dk.append(dot(grad_score, q, TN))
                dv.append(dot(prob.astype(BF), g, TN))
            for j, (got, scale) in enumerate(((dq, 0.125), (dk, 0.125), (dv, 1.0))):
                block = j * PAIRS + i
                qkv_o[block // per, :, span(block % per, PAIR)] = (
                    jnp.where(lane < HEAD, got[0], got[1]) * scale
                ).astype(BF)
            return c

        lax.fori_loop(0, PAIRS, attend, 0)
        put(0).start()
        in_copy.wait()
        part = 3 * WIDTH // SIDE
        back = dot(qkv_o[0], proj_in[:, :part], NT)
        for q in range(1, SIDE):
            back = back + dot(qkv_o[q], proj_in[:, q * part : (q + 1) * part], NT)
        normed, factor = normalize(stream[...])
        line_o[...] = jnp.broadcast_to(jnp.sum(back * normed, axis=0, keepdims=True), line_o.shape)
        back = grad_two[...] + norm_back(back * gain_one[...].astype(F32), normed, factor)
        stream_o[...] = back
        for q in range(SIDE):
            part = WIDTH // SIDE
            pool_o[q] = back[:, q * part : (q + 1) * part].astype(BF)
        for i in (1, 2, 3):
            put(i).start()
        for i in range(n):
            put(i).wait()


def attend_back(active, grad_two, qkv, lse, seg_c, seg_r, stream, gain_one, proj_in, proj_out, earlier):
    again = earlier is not None
    given = (active, grad_two, qkv, lse, seg_c, seg_r, stream, gain_one, proj_in, proj_out)
    return pl.pallas_call(
        partial(attend_back_kernel, again),
        out_shape=ATTEND_OUT,
        in_specs=[SM] + [VM] * 7 + [HB] * 2 + ([HB] * len(ATTEND_OUT) if again else []),
        out_specs=(HB,) * len(ATTEND_OUT),
        scratch_shapes=[pltpu.VMEM(o.shape, o.dtype) for o in ATTEND_OUT]
        + [
            pltpu.VMEM(proj_in.shape, BF),
            pltpu.VMEM(proj_out.shape, BF),
            pltpu.VMEM((ROWS, ROWS), F32),
            pltpu.VMEM((ROWS, WIDTH), BF),
            pltpu.SemaphoreType.DMA((2,)),
            pltpu.SemaphoreType.DMA((len(ATTEND_OUT),)),
        ],
        input_output_aliases={len(given) + i: i for i in range(len(ATTEND_OUT))} if again else {},
        compiler_params=pltpu.CompilerParams(vmem_limit_bytes=BIG),
        cost_estimate=pl.CostEstimate(flops=5 * 10**9, bytes_accessed=15 * 10**6, transcendentals=0),
    )(*given, *(earlier if again else ()))


def pool_back_kernel(branch, pool_w, patch, prob, value_t, value_o, score_o, mixed_t, blend):
    part = WIDTH // SIDE
    got = dot(pool_w[:, :part], branch[0], NT)
    for q in range(1, SIDE):
        got = got + dot(pool_w[:, q * part : (q + 1) * part], branch[q], NT)
    mixed_t[...] = got.astype(BF)
    lane = lax.broadcasted_iota(jnp.int32, (VARS, HEADS), 1)

    def head(h, c):
        rows = span(h, HEAD)
        back = dot(value_t[rows, :], mixed_t[rows, :], TN)
        grad_prob = back[PIX * VARS :]
        for p in range(PIX):
            grad_prob = grad_prob + back[p * VARS : (p + 1) * VARS] * patch[p]
        weight = prob[h]
        inner = jnp.sum(grad_prob * weight, axis=0, keepdims=True)
        grad_score = (weight * (grad_prob - inner)).astype(BF).astype(F32)
        for p in range(PIX + 1):
            lines = slice(p * VARS, (p + 1) * VARS)
            seen = grad_score if p == PIX else grad_score * patch[p]
            total = jnp.sum(seen, axis=-1, keepdims=True) * 0.125
            score_o[lines] = jnp.where(lane == h, total, score_o[lines])
            blend[lines] = (weight if p == PIX else weight * patch[p]).astype(BF)
        value_o[rows, :] = dot(mixed_t[rows, :], blend[...], NT).astype(BF)
        return c

    score_o[...] = jnp.zeros_like(score_o)
    lax.fori_loop(0, HEADS, head, 0)


def pool_back(branch, pool_w, patch, prob, value_t):
    return pl.pallas_call(
        pool_back_kernel,
        out_shape=(shape((WIDTH, KEYS), BF), shape((KEYS, HEADS), F32)),
        in_specs=[VM] * 5,
        out_specs=(VM, VM),
        scratch_shapes=[pltpu.VMEM((WIDTH, ROWS), BF), pltpu.VMEM((KEYS, ROWS), BF)],
        compiler_params=pltpu.CompilerParams(vmem_limit_bytes=BIG),
        cost_estimate=pl.CostEstimate(flops=2 * 10**9, bytes_accessed=5 * 10**6, transcendentals=0),
    )(branch, pool_w, patch, prob, value_t)


def term_kernel(count, offsets, *refs):
    left = refs[:count]
    right = [refs[count * (i + 1) : count * (i + 2)] for i in range(len(offsets))]
    out = refs[count * (len(offsets) + 1)]

    def block(i, c):
        for parts, (base, first, at, size) in zip(right, offsets):
            total = None
            for a, b in zip(left, parts):
                rows = pl.ds(pl.multiple_of(base + i * 256, 256), 256)
                got = dot(a[:, rows], b[:, first : first + size], TN)
                total = got if total is None else total + got
            out[span(i, 256), at : at + size] = total.astype(BF)
        return c

    lax.fori_loop(0, WIDTH // 256, block, 0)


def weight_term(left, rights, offsets):
    columns = sum(o[3] for o in offsets)
    return pl.pallas_call(
        partial(term_kernel, len(left), offsets),
        out_shape=shape((WIDTH, columns), BF),
        in_specs=[VM] * (len(left) * (1 + len(rights))),
        out_specs=VM,
        compiler_params=pltpu.CompilerParams(vmem_limit_bytes=BIG),
        cost_estimate=pl.CostEstimate(flops=2 * 10**9, bytes_accessed=5 * 10**6, transcendentals=0),
    )(*left, *[r for parts in rights for r in parts])


def local(
    tokens,
    pixels,
    segments,
    embed_weight,
    var_embed,
    var_query,
    query_weight,
    key_weight,
    value_weight,
    pool_weight,
    first_gain,
    project_in,
    project_out,
    second_gain,
    up_weight,
    up_bias,
    down_weight,
    down_bias,
    cotangent,
):
    section = lax.axis_index("section")
    is_first = section == 0
    micro, _, seq, width = tokens.shape
    rows = micro * seq
    value_w, query_w, key_w = value_weight[0], query_weight[0], key_weight[0]
    up_w, down_w, proj_in, proj_out, pool_w = (
        w[0] for w in (up_weight, down_weight, project_in, project_out, pool_weight)
    )
    table = jnp.concatenate(
        [embed_weight[0].transpose(1, 0, 2).reshape(PIX * VARS, width), var_embed[0]]
    )
    query_vec, probe, quick, value_t = prepare(table, var_query, query_w, key_w, value_w)
    patch = pixels[:, 0].astype(F32).transpose(2, 1, 0, 3).reshape(PIX, VARS, rows)
    seg_ids = (segments[:, 0] + SIDE * jnp.arange(micro)[:, None]).reshape(rows)
    seg_c, seg_r = seg_ids[:, None], seg_ids[None]
    inputs = tokens.reshape(rows, width)
    on_first = jnp.where(is_first, 1, 0).astype(jnp.int32).reshape(1)
    on_second = 1 - on_first

    base = (patch, seg_c, seg_r, quick, value_t)
    lines = (first_gain, second_gain, up_bias, down_bias)
    weights = (pool_w, proj_in, proj_out, up_w, down_w)
    saved = forward(on_first, inputs, base, lines, weights, None)
    passed = lax.ppermute(saved[0], "section", [(0, 1)])
    saved = forward(on_second, passed, base, lines, weights, saved)
    result, prob, stream, stream_two, qkv, lse, slope, for_x, for_y, for_z = saved

    all_x = share(for_x, "x")
    all_y = deal(for_y, "y", 0)
    all_z = share(for_z, "z")

    top_grad = cotangent.reshape(rows, width)
    low = mlp_back(on_second, top_grad, stream_two, slope, second_gain, up_w, down_w, None)
    high = attend_back(
        on_second, low[1], qkv, lse, seg_c, seg_r, stream, first_gain, proj_in, proj_out, None
    )
    passed = lax.ppermute(high[1].astype(BF), "section", [(1, 0)])
    branch_down = jnp.where(is_first, passed, top_grad)
    low = mlp_back(on_first, branch_down, stream_two, slope, second_gain, up_w, down_w, low)
    high = attend_back(
        on_first, low[1], qkv, lse, seg_c, seg_r, stream, first_gain, proj_in, proj_out, high
    )
    grad_pre, _, low_lines = low
    grad_qkv, grad_in, branch_pool, high_lines = high

    down_all = share(branch_down, "y")
    pre_all = deal(grad_pre, "x", 0)
    qkv_all = deal(grad_qkv, "z", 0)
    branch_all = deal(branch_pool, "z", 0)
    value_term, score_term = pool_back(branch_pool, pool_w, patch, prob, value_t)

    along_y = weight_term(down_all, [all_y], ((0, 0, 0, FF // SIDE),))
    along_x = weight_term(
        all_x,
        [pre_all, pre_all],
        ((0, 0, 0, FF // SIDE), (WIDTH, FF // SIDE, FF // SIDE, WIDTH // SIDE)),
    )
    along_z = weight_term(
        all_z,
        [qkv_all, branch_all],
        ((0, 0, 0, 3 * WIDTH // SIDE), (WIDTH, 0, 3 * WIDTH // SIDE, WIDTH // SIDE)),
    )

    chips = SIDE**3
    own = width // chips
    small = jnp.concatenate([score_term.reshape(-1), low_lines[:6].reshape(-1), high_lines[0]])
    small = small.astype(BF).reshape(chips, -1)
    used = own * KEYS + small.shape[1]
    every = jnp.concatenate(
        [
            value_term.reshape(chips, own * KEYS),
            small,
            jnp.zeros((chips, -used % 128), BF),
        ],
        axis=1,
    ).reshape(chips, -1, 128)
    every = lax.all_to_all(every, "batch", 0, 0, tiled=True)
    every = jnp.sum(every.astype(F32), axis=0, keepdims=True).astype(BF)
    every = jnp.broadcast_to(every, (chips,) + every.shape[1:])
    every = lax.all_to_all(every, "batch", 0, 0, tiled=True).reshape(chips, -1)

    def cube(value):
        return value.reshape(SIDE, SIDE, SIDE, -1, value.shape[-1])

    along_y = added(deal(cube(along_y), "z", 0)).astype(BF)
    along_x = added(deal(cube(along_x), "y", 1)).astype(BF)
    along_z = added(deal(cube(along_z), "x", 2)).astype(BF)
    along_y = added(deal(along_y, "x", 1)).astype(BF)
    along_x = added(deal(along_x, "z", 0)).astype(BF)
    along_z = added(deal(along_z, "y", 1)).astype(BF)
    along_y = set_back(deal(along_y, "y", 0), "y", 1).astype(F32)
    along_x = set_back(deal(along_x, "x", 0), "x", 1).astype(F32)
    along_z = set_back(deal(along_z, "z", 0), "z", 1).astype(F32)
    wide = FF // SIDE
    grad_up = along_x[..., :wide].reshape(own, -1)
    grad_out = along_x[..., wide:].reshape(own, -1)
    grad_down = along_y.reshape(own, -1).T
    wide = 3 * WIDTH // SIDE
    grad_in_w = along_z[..., :wide].reshape(own, -1)
    grad_pool = along_z[..., wide:].reshape(own, -1)

    value_sum = every[:, : own * KEYS].reshape(width, KEYS)
    small = every[:, own * KEYS : used].astype(F32).reshape(-1)
    score_sum = small[: KEYS * HEADS].reshape(KEYS, HEADS)
    found = small[KEYS * HEADS :]
    at = lax.axis_index("batch") * own
    mine = partial(lax.dynamic_slice_in_dim, start_index=at, slice_size=own)
    precise = partial(jnp.einsum, precision=lax.Precision.HIGHEST, preferred_element_type=F32)
    table_mine = mine(table, axis=1)
    grad_value = dot(table_mine, value_sum, ((0,), (1,)))
    grad_table = dot(value_sum, mine(value_w, axis=0), ((0,), (1,)))
    grad_table = grad_table + precise("kh,hd->kd", score_sum, mine(probe, axis=1))
    grad_probe = precise("kh,kd->hd", score_sum, table.astype(F32))
    crossed = dot(grad_probe.astype(BF), key_w, NN)
    grad_qvec = jnp.sum(
        jnp.where(
            jnp.arange(width)[None] // HEAD == jnp.arange(HEADS)[:, None],
            crossed,
            0.0,
        ),
        axis=0,
    )
    grad_key = (
        mine(grad_probe, axis=1).T[:, :, None] * query_vec.reshape(1, HEADS, HEAD)
    ).reshape(own, width)
    grad_qw = mine(var_query[0], axis=0).astype(F32)[:, None] * grad_qvec[None]
    grad_vq = jnp.sum(mine(query_w, axis=0).astype(F32) * grad_qvec[None], axis=1)
    grad_embed = grad_table[: PIX * VARS].reshape(PIX, VARS, own).transpose(1, 0, 2)
    grad_var = grad_table[PIX * VARS :]
    line_two = mine(found[:width], axis=0)
    line_down = mine(found[width : 2 * width], axis=0)
    line_up = lax.dynamic_slice_in_dim(found[2 * width : 6 * width], at * SIDE, own * SIDE)
    line_one = mine(found[6 * width :], axis=0)

    return (
        result.reshape(1, micro, 1, seq, width),
        grad_in.reshape(1, micro, 1, seq, width),
        grad_embed[None],
        grad_var[None],
        grad_vq[None],
        grad_qw[None],
        grad_key[None],
        grad_value[None],
        grad_pool[None],
        line_one[None],
        grad_in_w[None],
        grad_out[None],
        line_two[None],
        grad_up[None],
        line_up[None],
        grad_down[None],
        line_down[None],
    )


def solution(mesh):
    in_specs = (
        P(None, "batch", None, None),
        P(None, "batch", None, None, None),
        P(None, "batch", None),
        P("section", None, None, None),
        P("section", None, None),
        P("section", None),
        P("section", None, None),
        P("section", None, None),
        P("section", None, None),
        P("section", None, None),
        P("section", None),
        P("section", None, None),
        P("section", None, None),
        P("section", None),
        P("section", None, None),
        P("section", None),
        P("section", None, None),
        P("section", None),
        P(None, "batch", None, None),
    )
    out_specs = (
        P("section", None, "batch", None, None),
        P("section", None, "batch", None, None),
        P("section", None, None, "batch"),
        P("section", None, "batch"),
        P("section", "batch"),
        P("section", "batch", None),
        P("section", "batch", None),
        P("section", "batch", None),
        P("section", "batch", None),
        P("section", "batch"),
        P("section", "batch", None),
        P("section", "batch", None),
        P("section", "batch"),
        P("section", "batch", None),
        P("section", "batch"),
        P("section", None, "batch"),
        P("section", "batch"),
    )
    return jax.shard_map(local, mesh=mesh, in_specs=in_specs, out_specs=out_specs, check_vma=False)
```

```python
from functools import partial

import jax
import jax.numpy as jnp
from jax import lax
from jax.experimental import pallas as pl
from jax.experimental.pallas import tpu as pltpu
from jax.sharding import PartitionSpec as P

HEADS = 16
HEAD = 64
VARS = 48
PIX = 4
SIDE = 4
MASK_FILL = -1000000000.0
NORM_EPS = 1e-06
STRIDE = {"x": 1, "y": SIDE, "z": SIDE * SIDE}
BF = jnp.bfloat16
F32 = jnp.float32


def dot(a, b, contract):
    return lax.dot_general(a, b, (contract, ((), ())), preferred_element_type=F32)


def moved(axis, step):
    chips = SIDE**3
    pairs = []
    for section in (0, 1):
        signed = step if section == 0 else -step
        for chip in range(chips):
            at = (chip // STRIDE[axis]) % SIDE
            to = chip + ((at + signed) % SIDE - at) * STRIDE[axis]
            pairs.append((section * chips + chip, section * chips + to))
    return pairs


def swap(value, axis, step):
    return lax.ppermute(value, ("section", "batch"), moved(axis, step))


def place(axis):
    return (lax.axis_index("batch") // STRIDE[axis]) % SIDE


def share(value, axis):
    return [value] + [swap(value, axis, k) for k in (1, 2, 3)]


def handed(parts, axis):
    return [parts[0]] + [swap(parts[k], axis, k) for k in (1, 2, 3)]


VM = pl.BlockSpec(memory_space=pltpu.VMEM)
SM = pl.BlockSpec(memory_space=pltpu.SMEM)
HB = pl.BlockSpec(memory_space=pl.ANY)
BIG = 60 * 1024 * 1024
ROWS = 256
WIDTH = HEADS * HEAD
FF = 4096
TILE = 512
KEYS = (PIX + 1) * VARS
PAIR = 2 * HEAD
PAIRS = HEADS // 2
NN = ((1,), (0,))
NT = ((1,), (1,))
TN = ((0,), (0,))


def span(index, size):
    return pl.ds(pl.multiple_of(index * size, size), size)


def shape(dims, dtype):
    return jax.ShapeDtypeStruct(dims, dtype)


def prepare_kernel(table, var_q, query_w, key_w, value_w, query_vec, probe, quick, value_t):
    found = dot(jnp.broadcast_to(var_q[...], (16, WIDTH)), query_w[...], NN).astype(BF)
    query_vec[...] = found[0:1].astype(F32)
    head = lax.broadcasted_iota(jnp.int32, (16, WIDTH), 0)
    lane = lax.broadcasted_iota(jnp.int32, (16, WIDTH), 1)
    spread = jnp.where(lane // HEAD == head, found.astype(F32), 0.0).astype(BF)
    made = dot(spread, key_w[...], NT).astype(BF)
    probe[...] = made.astype(F32)
    quick[...] = dot(table[...], made, NT) * 0.125
    value_t[...] = dot(table[...], value_w[...], NN).T.astype(BF)


def prepare(table, var_q, query_w, key_w, value_w):
    return pl.pallas_call(
        prepare_kernel,
        out_shape=(
            shape((1, WIDTH), F32),
            shape((HEADS, WIDTH), F32),
            shape((KEYS, HEADS), F32),
            shape((WIDTH, KEYS), BF),
        ),
        in_specs=[VM] * 5,
        out_specs=(VM,) * 4,
        compiler_params=pltpu.CompilerParams(vmem_limit_bytes=BIG),
    )(table, var_q, query_w, key_w, value_w)


def normalize(value):
    center = value - jnp.mean(value, axis=-1, keepdims=True)
    factor = lax.rsqrt(jnp.mean(center * center, axis=-1, keepdims=True) + NORM_EPS)
    return (center * factor, factor)


def norm_back(grad, normed, factor):
    return factor * (
        grad
        - jnp.mean(grad, axis=-1, keepdims=True)
        - normed * jnp.mean(grad * normed, axis=-1, keepdims=True)
    )


def halves():
    lane = lax.broadcasted_iota(jnp.int32, (1, PAIR), 1)
    return [jnp.where(lane // HEAD == half, 1.0, 0.0).astype(BF) for half in (0, 1)]


def column(value, index):
    lane = lax.broadcasted_iota(jnp.int32, value.shape, 1)
    return jnp.sum(jnp.where(lane == index, value, 0.0), axis=-1, keepdims=True)


FORWARD_OUT = (
    shape((ROWS, WIDTH), BF),
    shape((HEADS, VARS, ROWS), F32),
    shape((ROWS, WIDTH), F32),
    shape((ROWS, WIDTH), F32),
    shape((ROWS, 3 * WIDTH), BF),
    shape((ROWS, 128), F32),
    shape((ROWS, FF), BF),
    shape((ROWS, 2 * WIDTH), BF),
    shape((ROWS, 2 * WIDTH), BF),
) + (shape((ROWS, FF // SIDE), BF),) * SIDE
FORWARD_HELD = FORWARD_OUT[:9] + (shape((SIDE, ROWS, FF // SIDE), BF),)


def forward_kernel(again, *refs):
    active, order = refs[:2]
    (inputs, patch, seg_c, seg_r, quick, value_t, gain_one, gain_two, up_b, down_b) = refs[2:12]
    weights = refs[12:17]
    refs = refs[17:]
    n = len(FORWARD_OUT)
    if again:
        refs = refs[n:]
    outs, held = refs[:n], refs[n : n + len(FORWARD_HELD)]
    refs = refs[n + len(FORWARD_HELD) :]
    pool_w, proj_in, proj_out, up_w, down_w = refs[:5]
    blend, mask, acc, w_sem, o_sem = refs[5:]
    result, prob_o, stream_o, two_o, qkv_o, lse_o, slope_o, for_x, for_z, for_y = held

    @pl.when(active[0] == 1)
    def _():
        def fetch(i):
            return pltpu.make_async_copy(
                weights[i], (pool_w, proj_in, proj_out, up_w, down_w)[i], w_sem.at[i]
            )

        def put(i):
            source = held[i] if i < 9 else for_y.at[order[4 + i - 9]]
            return pltpu.make_async_copy(source, outs[i], o_sem.at[i])

        for i in range(5):
            fetch(i).start()
        for pair in range(PAIRS):
            both = []
            for head in (2 * pair, 2 * pair + 1):
                score = quick[PIX * VARS :, head : head + 1] + jnp.zeros((VARS, ROWS), F32)
                for p in range(PIX):
                    score = score + quick[p * VARS : (p + 1) * VARS, head : head + 1] * patch[p]
                grown = jnp.exp(score - jnp.max(score, axis=0, keepdims=True))
                prob = grown / jnp.sum(grown, axis=0, keepdims=True)
                prob_o[head] = prob
                for p in range(PIX):
                    blend[p * VARS : (p + 1) * VARS] = (prob * patch[p]).astype(BF)
                blend[PIX * VARS :] = prob.astype(BF)
                both.append(dot(value_t[head * HEAD : (head + 1) * HEAD], blend[...], NN))
            at = WIDTH + pair * PAIR
            for_z[:, at : at + PAIR] = jnp.concatenate(both, axis=0).T.astype(BF)
        put(1).start()
        fetch(0).wait()
        stream = inputs[...].astype(F32) + dot(for_z[:, WIDTH:], pool_w[...], NN)
        stream_o[...] = stream
        put(2).start()
        normed, _ = normalize(stream)
        for_z[:, :WIDTH] = (normed * gain_one[...].astype(F32)).astype(BF)
        put(8).start()
        fetch(1).wait()

        def project(i, c):
            qkv_o[:, span(i, TILE)] = dot(for_z[:, :WIDTH], proj_in[:, span(i, TILE)], NN).astype(BF)
            return c

        lax.fori_loop(0, 3 * WIDTH // TILE, project, 0)
        put(4).start()
        mask[...] = jnp.where(seg_c[...] == seg_r[...], 1.0, 0.0)
        halfs = halves()
        lane = lax.broadcasted_iota(jnp.int32, (ROWS, 128), 1)

        def attend(i, lse):
            q = qkv_o[:, span(i, PAIR)]
            k = qkv_o[:, span(PAIRS + i, PAIR)]
            v = qkv_o[:, span(2 * PAIRS + i, PAIR)]
            got = []
            for half in (0, 1):
                raw = dot(q * halfs[half], k, NT) * 0.125
                score = jnp.where(mask[...] > 0.5, raw, MASK_FILL)
                top = jnp.max(score, axis=-1, keepdims=True)
                grown = jnp.exp(score - top)
                total = jnp.sum(grown, axis=-1, keepdims=True)
                lse = jnp.where(lane == 2 * i + half, top + jnp.log(total), lse)
                got.append(dot((grown / total).astype(BF), v, NN))
            for_x[:, span(PAIRS + i, PAIR)] = jnp.where(lane < HEAD, got[0], got[1]).astype(BF)
            return lse

        lse_o[...] = lax.fori_loop(0, PAIRS, attend, jnp.zeros((ROWS, 128), F32))
        put(5).start()
        fetch(2).wait()
        two = stream_o[...] + dot(for_x[:, WIDTH:], proj_out[...], NN)
        two_o[...] = two
        put(3).start()
        normed, _ = normalize(two)
        for_x[:, :WIDTH] = (normed * gain_two[...].astype(F32)).astype(BF)
        put(7).start()
        acc[...] = two + down_b[...].astype(F32)
        fetch(3).wait()
        fetch(4).wait()

        def mlp(i, c):
            pre = dot(for_x[:, :WIDTH], up_w[:, span(i, TILE)], NN) + up_b[:, span(i, TILE)].astype(F32)
            cdf = 0.5 * (1.0 + lax.erf(pre * 0.7071067811865476))
            slope_o[:, span(i, TILE)] = (
                cdf + pre * (jnp.exp(-0.5 * pre * pre) * 0.3989422804014327)
            ).astype(BF)
            hid = (pre * cdf).astype(BF)
            per = FF // SIDE // TILE
            for_y[i // per, :, span(i % per, TILE)] = hid
            acc[...] += dot(hid, down_w[span(i, TILE), :], NN)
            return c

        lax.fori_loop(0, FF // TILE, mlp, 0)
        result[...] = acc[...].astype(BF)
        for i in (0, 6, 9, 10, 11, 12):
            put(i).start()
        for i in range(n):
            put(i).wait()


def forward(active, order, inputs, base, lines, weights, earlier):
    again = earlier is not None
    given = (active, order, inputs, *base, *lines, *weights)
    return pl.pallas_call(
        partial(forward_kernel, again),
        out_shape=FORWARD_OUT,
        in_specs=[SM] * 2 + [VM] * 10 + [HB] * 5 + ([HB] * len(FORWARD_OUT) if again else []),
        out_specs=(HB,) * len(FORWARD_OUT),
        scratch_shapes=[pltpu.VMEM(o.shape, o.dtype) for o in FORWARD_HELD]
        + [pltpu.VMEM(w.shape, w.dtype) for w in weights]
        + [
            pltpu.VMEM((KEYS, ROWS), BF),
            pltpu.VMEM((ROWS, ROWS), F32),
            pltpu.VMEM((ROWS, WIDTH), F32),
            pltpu.SemaphoreType.DMA((5,)),
            pltpu.SemaphoreType.DMA((len(FORWARD_OUT),)),
        ],
        input_output_aliases={len(given) + i: i for i in range(len(FORWARD_OUT))} if again else {},
        compiler_params=pltpu.CompilerParams(vmem_limit_bytes=BIG),
        cost_estimate=pl.CostEstimate(flops=8 * 10**9, bytes_accessed=40 * 10**6, transcendentals=0),
    )(*given, *(earlier if again else ()))


MLP_OUT = (
    shape((ROWS, WIDTH), F32),
    shape((8, WIDTH), F32),
) + (shape((ROWS, (FF + WIDTH) // SIDE), BF),) * SIDE
MLP_HELD = MLP_OUT[:2] + (shape((SIDE, ROWS, (FF + WIDTH) // SIDE), BF),)


def mlp_back_kernel(again, after, *refs):
    active, order, grad, two, slope, gain_two, up_hbm, down_hbm = refs[:8]
    n = len(MLP_OUT)
    refs = refs[8 + after + (n if again else 0) :]
    outs, held = refs[:n], refs[n : n + 3]
    up_w, down_w, acc, w_sem, o_sem = refs[n + 3 :]
    two_o, line_o, pre_o = held

    @pl.when(active[0] == 1)
    def _():
        down_copy = pltpu.make_async_copy(down_hbm, down_w, w_sem.at[0])
        up_copy = pltpu.make_async_copy(up_hbm, up_w, w_sem.at[1])
        down_copy.start()
        up_copy.start()

        def put(i):
            source = held[i] if i < 2 else pre_o.at[order[i - 2]]
            return pltpu.make_async_copy(source, outs[i], o_sem.at[i])

        normed, factor = normalize(two[...])
        two_o[...] = normed
        acc[...] = jnp.zeros_like(acc)
        line_o[...] = jnp.zeros_like(line_o)
        down_copy.wait()
        up_copy.wait()
        per = FF // SIDE // TILE

        def mlp(i, c):
            hid = dot(grad[...], down_w[span(i, TILE), :], NT).astype(BF).astype(F32)
            pre = (hid * slope[:, span(i, TILE)].astype(F32)).astype(BF)
            pre_o[i // per, :, span(i % per, TILE)] = pre
            line_o[pl.ds(2 + i // per, 1), span(i % per, TILE)] = jnp.sum(
                pre.astype(F32), axis=0, keepdims=True
            )
            acc[...] += dot(pre, up_w[:, span(i, TILE)], NT)
            return c

        lax.fori_loop(0, FF // TILE, mlp, 0)
        normed = two_o[...]
        got = acc[...]
        line_o[0:1] = jnp.sum(got * normed, axis=0, keepdims=True)
        line_o[1:2] = jnp.sum(grad[...].astype(F32), axis=0, keepdims=True)
        back = grad[...].astype(F32) + norm_back(got * gain_two[...].astype(F32), normed, factor)
        two_o[...] = back
        for q in range(SIDE):
            part = WIDTH // SIDE
            pre_o[q, :, FF // SIDE :] = back[:, q * part : (q + 1) * part].astype(BF)
        for i in range(n):
            put(i).start()
        for i in range(n):
            put(i).wait()


def mlp_back(active, order, grad, two, slope, gain_two, up_w, down_w, after, earlier):
    again = earlier is not None
    given = (active, order, grad, two, slope, gain_two, up_w, down_w, *after)
    return pl.pallas_call(
        partial(mlp_back_kernel, again, len(after)),
        out_shape=MLP_OUT,
        in_specs=[SM] * 2
        + [VM] * 4
        + [HB] * (2 + len(after))
        + ([HB] * len(MLP_OUT) if again else []),
        out_specs=(HB,) * len(MLP_OUT),
        scratch_shapes=[pltpu.VMEM(o.shape, o.dtype) for o in MLP_HELD]
        + [
            pltpu.VMEM(up_w.shape, BF),
            pltpu.VMEM(down_w.shape, BF),
            pltpu.VMEM((ROWS, WIDTH), F32),
            pltpu.SemaphoreType.DMA((2,)),
            pltpu.SemaphoreType.DMA((len(MLP_OUT),)),
        ],
        input_output_aliases={len(given) + i: i for i in range(len(MLP_OUT))} if again else {},
        compiler_params=pltpu.CompilerParams(vmem_limit_bytes=BIG),
        cost_estimate=pl.CostEstimate(flops=5 * 10**9, bytes_accessed=25 * 10**6, transcendentals=0),
    )(*given, *(earlier if again else ()))


ATTEND_OUT = (
    (
        shape((ROWS, WIDTH), F32),
        shape((8, WIDTH), F32),
    )
    + (shape((ROWS, WIDTH), BF),) * SIDE
)
ATTEND_HELD = ATTEND_OUT[:2] + (shape((SIDE, ROWS, WIDTH), BF),)


def attend_back_kernel(again, after, through, *refs):
    active, order, grad_two, qkv, lse, seg_c, seg_r, stream, gain_one, in_hbm, out_hbm = refs[:11]
    n = len(ATTEND_OUT)
    refs = refs[11 + after + through + (n if again else 0) :]
    outs = refs[:n]
    refs = refs[n + through :]
    held = refs[:3]
    proj_in, proj_out, mask, given, w_sem, o_sem = refs[3:]
    stream_o, line_o, qkv_o = held

    @pl.when(active[0] == 1)
    def _():
        out_copy = pltpu.make_async_copy(out_hbm, proj_out, w_sem.at[0])
        in_copy = pltpu.make_async_copy(in_hbm, proj_in, w_sem.at[1])
        out_copy.start()
        in_copy.start()

        def put(i):
            source = held[i] if i < 2 else qkv_o.at[order[8 + i - 2]]
            return pltpu.make_async_copy(source, outs[i], o_sem.at[i])

        mask[...] = jnp.where(seg_c[...] == seg_r[...], 1.0, 0.0)
        halfs = halves()
        lane = lax.broadcasted_iota(jnp.int32, (ROWS, PAIR), 1)
        out_copy.wait()
        given[...] = dot(grad_two[...].astype(BF), proj_out[...], NT).astype(BF)
        per = 3 * WIDTH // SIDE // PAIR

        def attend(i, c):
            q = qkv[:, span(i, PAIR)]
            k = qkv[:, span(PAIRS + i, PAIR)]
            v = qkv[:, span(2 * PAIRS + i, PAIR)]
            g = given[:, span(i, PAIR)]
            dq, dk, dv = [], [], []
            for half in (0, 1):
                raw = dot(q * halfs[half], k, NT) * 0.125
                score = jnp.where(mask[...] > 0.5, raw, MASK_FILL)
                prob = jnp.exp(score - column(lse[...], 2 * i + half))
                grad_prob = dot(g * halfs[half], v, NT)
                inner = jnp.sum(grad_prob * prob, axis=-1, keepdims=True)
                grad_score = (prob * (grad_prob - inner)).astype(BF)
                dq.append(dot(grad_score, k, NN))
                dk.append(dot(grad_score, q, TN))
                dv.append(dot(prob.astype(BF), g, TN))
            for j, (got, scale) in enumerate(((dq, 0.125), (dk, 0.125), (dv, 1.0))):
                block = j * PAIRS + i
                qkv_o[block // per, :, span(block % per, PAIR)] = (
                    jnp.where(lane < HEAD, got[0], got[1]) * scale
                ).astype(BF)
            return c

        lax.fori_loop(0, PAIRS, attend, 0)
        in_copy.wait()
        part = 3 * WIDTH // SIDE
        back = dot(qkv_o[0, :, :part], proj_in[:, :part], NT)
        for q in range(1, SIDE):
            back = back + dot(qkv_o[q, :, :part], proj_in[:, q * part : (q + 1) * part], NT)
        normed, factor = normalize(stream[...])
        line_o[...] = jnp.broadcast_to(jnp.sum(back * normed, axis=0, keepdims=True), line_o.shape)
        back = grad_two[...] + norm_back(back * gain_one[...].astype(F32), normed, factor)
        stream_o[...] = back
        last = WIDTH // SIDE
        for q in range(SIDE):
            qkv_o[q, :, part:] = back[:, q * last : (q + 1) * last].astype(BF)
        for i in (2, 3, 4, 5, 0, 1):
            put(i).start()
        for i in range(n):
            put(i).wait()


def attend_back(active, order, grad_two, kept, gain_one, proj_in, proj_out, after, earlier, through):
    again = earlier is not None
    given = (active, order, grad_two, *kept, gain_one, proj_in, proj_out, *after)
    n = len(ATTEND_OUT)
    aliases = {len(given) + i: n + i for i in range(len(through))}
    if again:
        aliases |= {len(given) + len(through) + i: i for i in range(n)}
    found = pl.pallas_call(
        partial(attend_back_kernel, again, len(after), len(through)),
        out_shape=ATTEND_OUT + tuple(shape(t.shape, t.dtype) for t in through),
        in_specs=[SM] * 2
        + [VM] * 7
        + [HB] * (2 + len(after) + len(through))
        + ([HB] * n if again else []),
        out_specs=(HB,) * (n + len(through)),
        scratch_shapes=[pltpu.VMEM(o.shape, o.dtype) for o in ATTEND_HELD]
        + [
            pltpu.VMEM(proj_in.shape, BF),
            pltpu.VMEM(proj_out.shape, BF),
            pltpu.VMEM((ROWS, ROWS), F32),
            pltpu.VMEM((ROWS, WIDTH), BF),
            pltpu.SemaphoreType.DMA((2,)),
            pltpu.SemaphoreType.DMA((n,)),
        ],
        input_output_aliases=aliases,
        compiler_params=pltpu.CompilerParams(vmem_limit_bytes=BIG),
        cost_estimate=pl.CostEstimate(flops=5 * 10**9, bytes_accessed=15 * 10**6, transcendentals=0),
    )(*given, *through, *(earlier if again else ()))
    return found[:n], found[n:]


def gate_kernel(first, passed, top_grad, *refs):
    refs[-1][...] = jnp.where(first[0] == 1, passed[...].astype(F32), top_grad[...].astype(F32)).astype(BF)


def gate(first, passed, top_grad, after):
    return pl.pallas_call(
        gate_kernel,
        out_shape=shape(passed.shape, BF),
        in_specs=[SM, VM, VM] + [HB] * len(after),
        out_specs=VM,
    )(first, passed, top_grad, *after)


TERMS = WIDTH + KEYS + HEADS


def pool_back_kernel(
    grad, pool_w, patch, prob, value_t, table, value_w, key_w, probe, out, line, mixed_t, blend, values, scores
):
    mixed_t[...] = dot(pool_w[...], grad[...].astype(BF), NT).astype(BF)
    lane = lax.broadcasted_iota(jnp.int32, (VARS, HEADS), 1)

    def head(h, c):
        rows = span(h, HEAD)
        back = dot(value_t[rows, :], mixed_t[rows, :], TN)
        grad_prob = back[PIX * VARS :]
        for p in range(PIX):
            grad_prob = grad_prob + back[p * VARS : (p + 1) * VARS] * patch[p]
        weight = prob[h]
        inner = jnp.sum(grad_prob * weight, axis=0, keepdims=True)
        grad_score = (weight * (grad_prob - inner)).astype(BF).astype(F32)
        for p in range(PIX + 1):
            lines = slice(p * VARS, (p + 1) * VARS)
            seen = grad_score if p == PIX else grad_score * patch[p]
            total = jnp.sum(seen, axis=-1, keepdims=True) * 0.125
            scores[lines] = jnp.where(lane == h, total, scores[lines])
            blend[lines] = (weight if p == PIX else weight * patch[p]).astype(BF)
        values[rows, :] = dot(mixed_t[rows, :], blend[...], NT).astype(BF)
        return c

    scores[...] = jnp.zeros_like(scores)
    lax.fori_loop(0, HEADS, head, 0)
    score = scores[...].astype(BF)
    out[:, :WIDTH] = dot(table[...], values[...], ((0,), (1,))).astype(BF)
    embed = dot(value_w[...], values[...], NN) + dot(probe[...].astype(BF), score, ((0,), (1,)))
    probe_term = dot(table[...], score, TN)
    out[:, WIDTH:] = jnp.concatenate([embed, probe_term], axis=1).astype(BF)
    crossed = dot(probe_term.astype(BF), key_w[...], TN)
    row = lax.broadcasted_iota(jnp.int32, (HEADS, WIDTH), 0)
    col = lax.broadcasted_iota(jnp.int32, (HEADS, WIDTH), 1)
    line[...] = jnp.sum(jnp.where(col // HEAD == row, crossed, 0.0), axis=0, keepdims=True)


def pool_back(grad, pool_w, patch, prob, value_t, table, value_w, key_w, probe):
    return pl.pallas_call(
        pool_back_kernel,
        out_shape=(shape((WIDTH, TERMS), BF), shape((1, WIDTH), F32)),
        in_specs=[VM] * 9,
        out_specs=(VM, VM),
        scratch_shapes=[
            pltpu.VMEM((WIDTH, ROWS), BF),
            pltpu.VMEM((KEYS, ROWS), BF),
            pltpu.VMEM((WIDTH, KEYS), BF),
            pltpu.VMEM((KEYS, HEADS), F32),
        ],
        compiler_params=pltpu.CompilerParams(vmem_limit_bytes=BIG),
        cost_estimate=pl.CostEstimate(flops=3 * 10**9, bytes_accessed=12 * 10**6, transcendentals=0),
    )(grad, pool_w, patch, prob, value_t, table, value_w, key_w, probe)


def scatter_rows(stage, slots, block, value, axis):
    if axis == 2:
        stage[slots[block]] = value
    elif axis == 1:
        for y in range(SIDE):
            stage[slots[y], pl.ds(block * 64, 64), :] = value[y * 64 : (y + 1) * 64]
    else:
        for y in range(SIDE):
            for x in range(SIDE):
                at = y * 64 + x * 16
                stage[slots[x], pl.ds(block * 64 + y * 16, 16), :] = value[at : at + 16]


def term_kernel(count, offsets, axis, extra, tail, slots, *refs):
    left = refs[:count]
    right = [refs[count * (i + 1) : count * (i + 2)] for i in range(len(offsets))]
    refs = refs[count * (len(offsets) + 1) :]
    if extra:
        more, refs = refs[0], refs[1:]
    if tail:
        small, refs = refs[0], refs[1:]
    outs, (stage, sem) = refs[:SIDE], refs[SIDE:]
    own = [slots[axis * SIDE + i] for i in range(SIDE)]
    for block in range(SIDE):
        made = []
        for parts, (base, first, size) in zip(right, offsets):
            total = None
            for a, b in zip(left, parts):
                got = dot(
                    a[:, base + block * 256 : base + (block + 1) * 256],
                    b[:, first : first + size],
                    TN,
                )
                total = got if total is None else total + got
            made.append(total.astype(BF))
        if extra:
            made.append(more[block * 256 : (block + 1) * 256, extra[0] : extra[1]])
        made = made[0] if len(made) == 1 else jnp.concatenate(made, axis=1)
        scatter_rows(stage, own, block, made, axis)
    if tail:
        for k in range(SIDE):
            stage[k, WIDTH // SIDE :, :WIDTH] = small[...]
            stage[k, WIDTH // SIDE :, WIDTH:] = jnp.zeros((tail, stage.shape[2] - WIDTH), BF)
    copies = [pltpu.make_async_copy(stage.at[k], outs[k], sem.at[k]) for k in range(SIDE)]
    for c in copies:
        c.start()
    for c in copies:
        c.wait()


def weight_term(slots, left, rights, offsets, axis, extra=None, more=None, small=None):
    columns = sum(o[2] for o in offsets) + (extra[1] - extra[0] if extra else 0)
    tail = 0 if small is None else small.shape[0]
    out = shape((WIDTH // SIDE + tail, columns), BF)
    given = [*left, *[r for parts in rights for r in parts]]
    given += [more] if extra else []
    given += [small] if tail else []
    return pl.pallas_call(
        partial(term_kernel, len(left), offsets, axis, extra, tail),
        out_shape=(out,) * SIDE,
        in_specs=[SM] + [VM] * len(given),
        out_specs=(HB,) * SIDE,
        scratch_shapes=[pltpu.VMEM((SIDE,) + out.shape, BF), pltpu.SemaphoreType.DMA((SIDE,))],
        compiler_params=pltpu.CompilerParams(vmem_limit_bytes=BIG),
        cost_estimate=pl.CostEstimate(flops=2 * 10**9, bytes_accessed=5 * 10**6, transcendentals=0),
    )(slots, *given)


def add_kernel(axis, inner, tail, slots, a, b, c, d, *refs):
    outs, (stage, sem) = refs[:SIDE], refs[SIDE:]
    rows = a.shape[0] - tail
    part = rows // SIDE
    total = a[...].astype(F32) + b[...].astype(F32) + c[...].astype(F32) + d[...].astype(F32)
    total = total.astype(BF)
    for i in range(SIDE):
        slot = slots[axis * SIDE + i]
        if inner:
            for j in range(SIDE):
                at = (j * SIDE + i) * 16
                stage[slot, j * 16 : (j + 1) * 16, :] = total[at : at + 16]
        else:
            stage[slot, :part, :] = total[i * part : (i + 1) * part]
        if tail:
            stage[slot, part:, :] = total[rows:]
    copies = [pltpu.make_async_copy(stage.at[k], outs[k], sem.at[k]) for k in range(SIDE)]
    for c in copies:
        c.start()
    for c in copies:
        c.wait()


def add_up(slots, pieces, axis, inner, tail=0):
    rows, columns = pieces[0].shape
    out = shape(((rows - tail) // SIDE + tail, columns), BF)
    return pl.pallas_call(
        partial(add_kernel, axis, inner, tail),
        out_shape=(out,) * SIDE,
        in_specs=[SM] + [VM] * 4,
        out_specs=(HB,) * SIDE,
        scratch_shapes=[pltpu.VMEM((SIDE,) + out.shape, BF), pltpu.SemaphoreType.DMA((SIDE,))],
        compiler_params=pltpu.CompilerParams(vmem_limit_bytes=BIG),
        cost_estimate=pl.CostEstimate(flops=10**6, bytes_accessed=5 * 10**6, transcendentals=0),
    )(slots, *pieces)


def last_kernel(half, order, *refs):
    xs, ys, zs = refs[:4], refs[4:8], refs[8:12]
    query_vec, var_q, query_w = refs[12:15]
    up, out, down, into, pool, value, embed, key, qweight, vquery, lines = refs[15:]
    wide, narrow, third = FF // SIDE, WIDTH // SIDE, 3 * WIDTH // SIDE
    own = up.shape[0]
    total_x = total_y = small = 0.0
    for k in range(SIDE):
        back = (SIDE - k) % SIDE
        q = order[back]
        up[:, span(q, wide)] = xs[k][:own, :wide].astype(F32)
        out[:, span(q, narrow)] = xs[k][:own, wide : wide + narrow].astype(F32)
        q = order[4 + back]
        down[span(q, wide), :] = ys[k][:, :wide].astype(F32).T
        q = order[8 + back]
        into[:, span(q, third)] = zs[k][:, :third].astype(F32)
        pool[:, span(q, narrow)] = zs[k][:, third:].astype(F32)
        total_x = total_x + xs[k][:own, wide + narrow :].astype(F32)
        total_y = total_y + ys[k][:, wide:].astype(F32)
        small = small + xs[k][own:, :WIDTH].astype(F32)
    total = jnp.concatenate([total_y, total_x], axis=1)
    value[...] = total[:, :WIDTH]
    embed[...] = total[:, WIDTH : WIDTH + KEYS].T
    row = lax.broadcasted_iota(jnp.int32, (HEADS, WIDTH), 0)
    col = lax.broadcasted_iota(jnp.int32, (HEADS, WIDTH), 1)
    spread = jnp.where(col // HEAD == row, 1.0, 0.0)
    probe = jnp.dot(
        total[:, WIDTH + KEYS :],
        spread,
        precision=lax.Precision.HIGHEST,
        preferred_element_type=F32,
    )
    key[...] = probe * query_vec[...]
    qvec = small[0:1]
    qweight[...] = var_q[...] * qvec
    vquery[...] = jnp.sum(query_w[...].astype(F32) * qvec, axis=1, keepdims=True)
    lines[...] = small


def last_step(order, xs, ys, zs, query_vec, var_q, query_w, half):
    own = WIDTH // SIDE**3
    return pl.pallas_call(
        partial(last_kernel, half),
        out_shape=(
            shape((own, FF), F32),
            shape((own, WIDTH), F32),
            shape((FF, own), F32),
            shape((own, 3 * WIDTH), F32),
            shape((own, WIDTH), F32),
            shape((own, WIDTH), F32),
            shape((KEYS, own), F32),
            shape((own, WIDTH), F32),
            shape((own, WIDTH), F32),
            shape((own, 1), F32),
            shape((own, WIDTH), F32),
        ),
        in_specs=[SM] + [VM] * 15,
        out_specs=(VM,) * 11,
        compiler_params=pltpu.CompilerParams(vmem_limit_bytes=BIG),
    )(order, *xs, *ys, *zs, query_vec, var_q, query_w)


def local(
    tokens,
    pixels,
    segments,
    embed_weight,
    var_embed,
    var_query,
    query_weight,
    key_weight,
    value_weight,
    pool_weight,
    first_gain,
    project_in,
    project_out,
    second_gain,
    up_weight,
    up_bias,
    down_weight,
    down_bias,
    cotangent,
):
    section = lax.axis_index("section")
    is_first = section == 0
    micro, _, seq, width = tokens.shape
    rows = micro * seq
    value_w, query_w, key_w = value_weight[0], query_weight[0], key_weight[0]
    up_w, down_w, proj_in, proj_out, pool_w = (
        w[0] for w in (up_weight, down_weight, project_in, project_out, pool_weight)
    )
    table = jnp.concatenate(
        [embed_weight[0].transpose(1, 0, 2).reshape(PIX * VARS, width), var_embed[0]]
    )
    query_vec, probe, quick, value_t = prepare(table, var_query, query_w, key_w, value_w)
    patch = pixels[:, 0].astype(F32).transpose(2, 1, 0, 3).reshape(PIX, VARS, rows)
    seg_ids = (segments[:, 0] + SIDE * jnp.arange(micro)[:, None]).reshape(rows)
    seg_c, seg_r = seg_ids[:, None], seg_ids[None]
    inputs = tokens.reshape(rows, width)
    on_first = jnp.where(is_first, 1, 0).astype(jnp.int32).reshape(1)
    on_second = 1 - on_first

    sign = jnp.where(is_first, 1, -1)
    steps = jnp.arange(SIDE)
    spots = [place(axis) for axis in "xyz"]
    order = jnp.concatenate([(at + sign * steps) % SIDE for at in spots]).astype(jnp.int32)
    slots = jnp.concatenate([(sign * (steps - at)) % SIDE for at in spots]).astype(jnp.int32)

    base = (patch, seg_c, seg_r, quick, value_t)
    lines = (first_gain, second_gain, up_bias, down_bias)
    weights = (pool_w, proj_in, proj_out, up_w, down_w)
    saved = forward(on_first, order, inputs, base, lines, weights, None)
    passed = lax.ppermute(saved[0], "section", [(0, 1)])
    saved = forward(on_second, order, passed, base, lines, weights, saved)
    result, prob, stream, stream_two, qkv, lse, slope, for_x, for_z = saved[:9]
    hidden = saved[9:]
    kept = (qkv, lse, seg_c, seg_r, stream)

    top_grad = cotangent.reshape(rows, width)
    low = mlp_back(
        on_second, order, top_grad, stream_two, slope, second_gain, up_w, down_w, (), None
    )
    all_x = share(for_x, "x")
    first_z = [swap(for_z, "z", k) for k in (1, 3)]
    high, (for_z, *hidden) = attend_back(
        on_second,
        order,
        low[0],
        kept,
        first_gain,
        proj_in,
        proj_out,
        (*all_x[1:], *first_z),
        None,
        (for_z, *hidden),
    )
    passed = lax.ppermute(high[0].astype(BF), "section", [(1, 0)])
    all_z = [for_z, first_z[0], swap(for_z, "z", 2), first_z[1]]
    all_y = handed(hidden, "y")
    branch_down = gate(on_first, passed, top_grad, (*all_y[1:], all_z[2]))
    down_all = share(branch_down, "y")
    low = mlp_back(
        on_first, order, branch_down, stream_two, slope, second_gain, up_w, down_w, (), low
    )
    high, _ = attend_back(
        on_first, order, low[0], kept, first_gain, proj_in, proj_out, tuple(down_all[1:]), high, ()
    )
    low_lines, grad_pre = low[1], low[2:]
    grad_in, high_lines, grad_qkv = high[0], high[1], high[2:]

    pre_all = handed(grad_pre, "x")
    qkv_all = handed(grad_qkv, "z")
    more, qvec_term = pool_back(
        grad_in, pool_w, patch, prob, value_t, table, value_w, key_w, probe
    )
    small = jnp.concatenate(
        [qvec_term, low_lines[:6], high_lines[:1], jnp.zeros((8, width), F32)]
    ).astype(BF)

    wide, narrow, third = FF // SIDE, WIDTH // SIDE, 3 * WIDTH // SIDE
    half = TERMS // 2
    ys = weight_term(slots, down_all, [all_y], ((0, 0, wide),), 2, (0, half), more)
    xs = weight_term(
        slots,
        all_x,
        [pre_all, pre_all],
        ((0, 0, wide), (WIDTH, wide, narrow)),
        1,
        (half, TERMS),
        more,
        small,
    )
    zs = weight_term(slots, all_z, [qkv_all, qkv_all], ((0, 0, third), (WIDTH, third, narrow)), 0)
    tail = small.shape[0]
    ys = add_up(slots, handed(ys, "z"), 0, True)
    xs = add_up(slots, handed(xs, "y"), 2, False, tail)
    zs = add_up(slots, handed(zs, "x"), 1, True)
    ys = add_up(slots, handed(ys, "x"), 1, False)
    xs = add_up(slots, handed(xs, "z"), 0, False, tail)
    zs = add_up(slots, handed(zs, "y"), 2, False)
    own = width // SIDE**3
    at = lax.axis_index("batch") * own
    mine = partial(lax.dynamic_slice_in_dim, start_index=at, slice_size=own)
    (
        grad_up,
        grad_out,
        grad_down,
        grad_in_w,
        grad_pool,
        grad_value,
        grad_table,
        grad_key,
        grad_qw,
        grad_vq,
        found,
    ) = last_step(
        order,
        handed(xs, "x"),
        handed(ys, "y"),
        handed(zs, "z"),
        query_vec,
        mine(var_query[0], axis=0).astype(F32)[:, None],
        mine(query_w, axis=0),
        half,
    )
    grad_vq = grad_vq[:, 0]
    grad_embed = grad_table[: PIX * VARS].reshape(PIX, VARS, own).transpose(1, 0, 2)
    grad_var = grad_table[PIX * VARS :]
    line_two = mine(found[1], axis=0)
    line_down = mine(found[2], axis=0)
    line_up = lax.dynamic_slice_in_dim(found[3:7].reshape(-1), at * SIDE, own * SIDE)
    line_one = mine(found[7], axis=0)

    return (
        result.reshape(1, micro, 1, seq, width),
        grad_in.reshape(1, micro, 1, seq, width),
        grad_embed[None],
        grad_var[None],
        grad_vq[None],
        grad_qw[None],
        grad_key[None],
        grad_value[None],
        grad_pool[None],
        line_one[None],
        grad_in_w[None],
        grad_out[None],
        line_two[None],
        grad_up[None],
        line_up[None],
        grad_down[None],
        line_down[None],
    )


def solution(mesh):
    in_specs = (
        P(None, "batch", None, None),
        P(None, "batch", None, None, None),
        P(None, "batch", None),
        P("section", None, None, None),
        P("section", None, None),
        P("section", None),
        P("section", None, None),
        P("section", None, None),
        P("section", None, None),
        P("section", None, None),
        P("section", None),
        P("section", None, None),
        P("section", None, None),
        P("section", None),
        P("section", None, None),
        P("section", None),
        P("section", None, None),
        P("section", None),
        P(None, "batch", None, None),
    )
    out_specs = (
        P("section", None, "batch", None, None),
        P("section", None, "batch", None, None),
        P("section", None, None, "batch"),
        P("section", None, "batch"),
        P("section", "batch"),
        P("section", "batch", None),
        P("section", "batch", None),
        P("section", "batch", None),
        P("section", "batch", None),
        P("section", "batch"),
        P("section", "batch", None),
        P("section", "batch", None),
        P("section", "batch"),
        P("section", "batch", None),
        P("section", "batch"),
        P("section", None, "batch"),
        P("section", "batch"),
    )
    return jax.shard_map(local, mesh=mesh, in_specs=in_specs, out_specs=out_specs, check_vma=False)
```

```python
from functools import partial

import jax
import jax.numpy as jnp
from jax import lax
from jax.experimental import pallas as pl
from jax.experimental.pallas import tpu as pltpu
from jax.sharding import PartitionSpec as P

HEADS = 16
HEAD = 64
VARS = 48
PIX = 4
SIDE = 4
MASK_FILL = -1000000000.0
NORM_EPS = 1e-06
STRIDE = {"x": 1, "y": SIDE, "z": SIDE * SIDE}
BF = jnp.bfloat16
F32 = jnp.float32


def dot(a, b, contract):
    return lax.dot_general(a, b, (contract, ((), ())), preferred_element_type=F32)


def moved(axis, step):
    chips = SIDE**3
    pairs = []
    for section in (0, 1):
        signed = step if section == 0 else -step
        for chip in range(chips):
            at = (chip // STRIDE[axis]) % SIDE
            to = chip + ((at + signed) % SIDE - at) * STRIDE[axis]
            pairs.append((section * chips + chip, section * chips + to))
    return pairs


def swap(value, axis, step):
    return lax.ppermute(value, ("section", "batch"), moved(axis, step))


def place(axis):
    return (lax.axis_index("batch") // STRIDE[axis]) % SIDE


def share(value, axis):
    return [value] + [swap(value, axis, k) for k in (1, 2, 3)]


def handed(parts, axis):
    return [parts[0]] + [swap(parts[k], axis, k) for k in (1, 2, 3)]


VM = pl.BlockSpec(memory_space=pltpu.VMEM)
SM = pl.BlockSpec(memory_space=pltpu.SMEM)
HB = pl.BlockSpec(memory_space=pl.ANY)
BIG = 60 * 1024 * 1024
ROWS = 256
WIDTH = HEADS * HEAD
FF = 4096
TILE = 1024
KEYS = (PIX + 1) * VARS
PAIR = 2 * HEAD
PAIRS = HEADS // 2
NN = ((1,), (0,))
NT = ((1,), (1,))
TN = ((0,), (0,))


def span(index, size):
    return pl.ds(pl.multiple_of(index * size, size), size)


def shape(dims, dtype):
    return jax.ShapeDtypeStruct(dims, dtype)


def prepare_kernel(
    table, var_q, query_hbm, key_hbm, value_hbm, query_vec, probe, quick, value_t, query_w, key_w, value_w, sem
):
    copies = [
        pltpu.make_async_copy(source, target, sem.at[i])
        for i, (source, target) in enumerate(
            ((value_hbm, value_w), (query_hbm, query_w), (key_hbm, key_w))
        )
    ]
    for copy in copies:
        copy.start()
    copies[0].wait()
    value_t[...] = dot(table[...], value_w[...], NN).T.astype(BF)
    copies[1].wait()
    found = dot(jnp.broadcast_to(var_q[...], (16, WIDTH)), query_w[...], NN).astype(BF)
    query_vec[...] = found[0:1].astype(F32)
    head = lax.broadcasted_iota(jnp.int32, (16, WIDTH), 0)
    lane = lax.broadcasted_iota(jnp.int32, (16, WIDTH), 1)
    spread = jnp.where(lane // HEAD == head, found.astype(F32), 0.0).astype(BF)
    copies[2].wait()
    made = dot(spread, key_w[...], NT).astype(BF)
    probe[...] = made.astype(F32)
    quick[...] = dot(table[...], made, NT) * 0.125


def prepare(table, var_q, query_w, key_w, value_w):
    return pl.pallas_call(
        prepare_kernel,
        out_shape=(
            shape((1, WIDTH), F32),
            shape((HEADS, WIDTH), F32),
            shape((KEYS, HEADS), F32),
            shape((WIDTH, KEYS), BF),
        ),
        in_specs=[VM] * 2 + [HB] * 3,
        out_specs=(VM,) * 4,
        scratch_shapes=[pltpu.VMEM(w.shape, BF) for w in (query_w, key_w, value_w)]
        + [pltpu.SemaphoreType.DMA((3,))],
        compiler_params=pltpu.CompilerParams(vmem_limit_bytes=BIG),
    )(table, var_q, query_w, key_w, value_w)


def normalize(value):
    center = value - jnp.mean(value, axis=-1, keepdims=True)
    factor = lax.rsqrt(jnp.mean(center * center, axis=-1, keepdims=True) + NORM_EPS)
    return (center * factor, factor)


def norm_back(grad, normed, factor):
    return factor * (
        grad
        - jnp.mean(grad, axis=-1, keepdims=True)
        - normed * jnp.mean(grad * normed, axis=-1, keepdims=True)
    )


def halves():
    lane = lax.broadcasted_iota(jnp.int32, (1, PAIR), 1)
    return [jnp.where(lane // HEAD == half, 1.0, 0.0).astype(BF) for half in (0, 1)]


def column(value, index):
    lane = lax.broadcasted_iota(jnp.int32, value.shape, 1)
    return jnp.sum(jnp.where(lane == index, value, 0.0), axis=-1, keepdims=True)


FORWARD_OUT = (
    shape((ROWS, WIDTH), BF),
    shape((HEADS, VARS, ROWS), F32),
    shape((ROWS, WIDTH), F32),
    shape((ROWS, WIDTH), F32),
    shape((ROWS, 3 * WIDTH), BF),
    shape((ROWS, 128), F32),
    shape((ROWS, FF), BF),
    shape((ROWS, 2 * WIDTH), BF),
    shape((ROWS, 2 * WIDTH), BF),
) + (shape((ROWS, FF // SIDE), BF),) * SIDE
FORWARD_HELD = FORWARD_OUT[:9] + (shape((SIDE, ROWS, FF // SIDE), BF),)


def forward_kernel(again, *refs):
    active, order = refs[:2]
    (inputs, patch, seg_c, seg_r, quick, value_t, gain_one, gain_two, up_b, down_b) = refs[2:12]
    weights = refs[12:17]
    refs = refs[17:]
    n = len(FORWARD_OUT)
    if again:
        refs = refs[n:]
    outs, held = refs[:n], refs[n : n + len(FORWARD_HELD)]
    refs = refs[n + len(FORWARD_HELD) :]
    pool_w, proj_in, proj_out, up_w, down_w = refs[:5]
    blend, mask, acc, w_sem, o_sem = refs[5:]
    result, prob_o, stream_o, two_o, qkv_o, lse_o, slope_o, for_x, for_z, for_y = held

    @pl.when(active[0] == 1)
    def _():
        def fetch(i):
            return pltpu.make_async_copy(
                weights[i], (pool_w, proj_in, proj_out, up_w, down_w)[i], w_sem.at[i]
            )

        def put(i):
            source = held[i] if i < 9 else for_y.at[order[4 + i - 9]]
            return pltpu.make_async_copy(source, outs[i], o_sem.at[i])

        for i in range(5):
            fetch(i).start()
        for pair in range(PAIRS):
            both = []
            for head in (2 * pair, 2 * pair + 1):
                score = quick[PIX * VARS :, head : head + 1] + jnp.zeros((VARS, ROWS), F32)
                for p in range(PIX):
                    score = score + quick[p * VARS : (p + 1) * VARS, head : head + 1] * patch[p]
                grown = jnp.exp(score - jnp.max(score, axis=0, keepdims=True))
                prob = grown / jnp.sum(grown, axis=0, keepdims=True)
                prob_o[head] = prob
                for p in range(PIX):
                    blend[p * VARS : (p + 1) * VARS] = (prob * patch[p]).astype(BF)
                blend[PIX * VARS :] = prob.astype(BF)
                both.append(dot(value_t[head * HEAD : (head + 1) * HEAD], blend[...], NN))
            at = WIDTH + pair * PAIR
            for_z[:, at : at + PAIR] = jnp.concatenate(both, axis=0).T.astype(BF)
        put(1).start()
        fetch(0).wait()
        stream = inputs[...].astype(F32) + dot(for_z[:, WIDTH:], pool_w[...], NN)
        stream_o[...] = stream
        put(2).start()
        normed, _ = normalize(stream)
        for_z[:, :WIDTH] = (normed * gain_one[...].astype(F32)).astype(BF)
        put(8).start()
        fetch(1).wait()

        def project(i, c):
            qkv_o[:, span(i, TILE)] = dot(for_z[:, :WIDTH], proj_in[:, span(i, TILE)], NN).astype(BF)
            return c

        lax.fori_loop(0, 3 * WIDTH // TILE, project, 0)
        put(4).start()
        mask[...] = jnp.where(seg_c[...] == seg_r[...], 1.0, 0.0)
        halfs = halves()
        lane = lax.broadcasted_iota(jnp.int32, (ROWS, 128), 1)

        def attend(i, lse):
            q = qkv_o[:, span(i, PAIR)]
            k = qkv_o[:, span(PAIRS + i, PAIR)]
            v = qkv_o[:, span(2 * PAIRS + i, PAIR)]
            got = []
            for half in (0, 1):
                raw = dot(q * halfs[half], k, NT) * 0.125
                score = jnp.where(mask[...] > 0.5, raw, MASK_FILL)
                top = jnp.max(score, axis=-1, keepdims=True)
                grown = jnp.exp(score - top)
                total = jnp.sum(grown, axis=-1, keepdims=True)
                lse = jnp.where(lane == 2 * i + half, top + jnp.log(total), lse)
                got.append(dot((grown / total).astype(BF), v, NN))
            for_x[:, span(PAIRS + i, PAIR)] = jnp.where(lane < HEAD, got[0], got[1]).astype(BF)
            return lse

        lse_o[...] = lax.fori_loop(0, PAIRS, attend, jnp.zeros((ROWS, 128), F32), unroll=True)
        put(5).start()
        fetch(2).wait()
        two = stream_o[...] + dot(for_x[:, WIDTH:], proj_out[...], NN)
        two_o[...] = two
        put(3).start()
        normed, _ = normalize(two)
        for_x[:, :WIDTH] = (normed * gain_two[...].astype(F32)).astype(BF)
        put(7).start()
        acc[...] = two + down_b[...].astype(F32)
        fetch(3).wait()
        fetch(4).wait()

        def mlp(i, c):
            pre = dot(for_x[:, :WIDTH], up_w[:, span(i, TILE)], NN) + up_b[:, span(i, TILE)].astype(F32)
            cdf = 0.5 * (1.0 + lax.erf(pre * 0.7071067811865476))
            slope_o[:, span(i, TILE)] = (
                cdf + pre * (jnp.exp(-0.5 * pre * pre) * 0.3989422804014327)
            ).astype(BF)
            hid = (pre * cdf).astype(BF)
            per = FF // SIDE // TILE
            for_y[i // per, :, span(i % per, TILE)] = hid
            acc[...] += dot(hid, down_w[span(i, TILE), :], NN)
            return c

        lax.fori_loop(0, FF // TILE, mlp, 0, unroll=True)
        result[...] = acc[...].astype(BF)
        for i in (0, 6, 9, 10, 11, 12):
            put(i).start()
        for i in range(n):
            put(i).wait()


def forward(active, order, inputs, base, lines, weights, earlier):
    again = earlier is not None
    given = (active, order, inputs, *base, *lines, *weights)
    return pl.pallas_call(
        partial(forward_kernel, again),
        out_shape=FORWARD_OUT,
        in_specs=[SM] * 2 + [VM] * 10 + [HB] * 5 + ([HB] * len(FORWARD_OUT) if again else []),
        out_specs=(HB,) * len(FORWARD_OUT),
        scratch_shapes=[pltpu.VMEM(o.shape, o.dtype) for o in FORWARD_HELD]
        + [pltpu.VMEM(w.shape, w.dtype) for w in weights]
        + [
            pltpu.VMEM((KEYS, ROWS), BF),
            pltpu.VMEM((ROWS, ROWS), F32),
            pltpu.VMEM((ROWS, WIDTH), F32),
            pltpu.SemaphoreType.DMA((5,)),
            pltpu.SemaphoreType.DMA((len(FORWARD_OUT),)),
        ],
        input_output_aliases={len(given) + i: i for i in range(len(FORWARD_OUT))} if again else {},
        compiler_params=pltpu.CompilerParams(vmem_limit_bytes=BIG),
        cost_estimate=pl.CostEstimate(flops=8 * 10**9, bytes_accessed=40 * 10**6, transcendentals=0),
    )(*given, *(earlier if again else ()))


MLP_OUT = (
    shape((ROWS, WIDTH), F32),
    shape((8, WIDTH), F32),
) + (shape((ROWS, (FF + WIDTH) // SIDE), BF),) * SIDE
MLP_HELD = MLP_OUT[:2] + (shape((SIDE, ROWS, (FF + WIDTH) // SIDE), BF),)


def mlp_back_kernel(again, after, *refs):
    active, order, grad, two_hbm, slope_hbm, gain_two, up_hbm, down_hbm = refs[:8]
    n = len(MLP_OUT)
    refs = refs[8 + after + (n if again else 0) :]
    outs, held = refs[:n], refs[n : n + 3]
    up_w, down_w, slope, two, acc, w_sem, o_sem = refs[n + 3 :]
    two_o, line_o, pre_o = held
    tiles = FF // TILE

    @pl.when(active[0] == 1)
    def _():
        fetches = []
        for i in range(tiles):
            at = pl.ds(i * TILE, TILE)
            fetches.append(
                [
                    pltpu.make_async_copy(down_hbm.at[at, :], down_w.at[at, :], w_sem.at[3 * i]),
                    pltpu.make_async_copy(slope_hbm.at[:, at], slope.at[:, at], w_sem.at[3 * i + 1]),
                    pltpu.make_async_copy(up_hbm.at[:, at], up_w.at[:, at], w_sem.at[3 * i + 2]),
                ]
            )
        fetch_two = pltpu.make_async_copy(two_hbm, two, w_sem.at[3 * tiles])
        for fetch in fetches:
            for copy in fetch:
                copy.start()
        fetch_two.start()

        def put(i):
            source = held[i] if i < 2 else pre_o.at[order[i - 2]]
            return pltpu.make_async_copy(source, outs[i], o_sem.at[i])

        line_o[...] = jnp.zeros_like(line_o)
        per = FF // SIDE // TILE
        for i in range(tiles):
            for copy in fetches[i]:
                copy.wait()
            at = slice(i * TILE, (i + 1) * TILE)
            inner = slice((i % per) * TILE, (i % per + 1) * TILE)
            hid = dot(grad[...], down_w[at, :], NT).astype(BF).astype(F32)
            pre = (hid * slope[:, at].astype(F32)).astype(BF)
            pre_o[i // per, :, inner] = pre
            line_o[2 + i // per : 3 + i // per, inner] = jnp.sum(
                pre.astype(F32), axis=0, keepdims=True
            )
            got = dot(pre, up_w[:, at], NT)
            acc[...] = got if i == 0 else acc[...] + got
        fetch_two.wait()
        normed, factor = normalize(two[...])
        got = acc[...]
        line_o[0:1] = jnp.sum(got * normed, axis=0, keepdims=True)
        line_o[1:2] = jnp.sum(grad[...].astype(F32), axis=0, keepdims=True)
        back = grad[...].astype(F32) + norm_back(got * gain_two[...].astype(F32), normed, factor)
        two_o[...] = back
        for q in range(SIDE):
            part = WIDTH // SIDE
            pre_o[q, :, FF // SIDE :] = back[:, q * part : (q + 1) * part].astype(BF)
        for i in range(n):
            put(i).start()
        for i in range(n):
            put(i).wait()


def mlp_back(active, order, grad, two, slope, gain_two, up_w, down_w, after, earlier):
    again = earlier is not None
    given = (active, order, grad, two, slope, gain_two, up_w, down_w, *after)
    return pl.pallas_call(
        partial(mlp_back_kernel, again, len(after)),
        out_shape=MLP_OUT,
        in_specs=[SM] * 2
        + [VM, HB, HB, VM]
        + [HB] * (2 + len(after))
        + ([HB] * len(MLP_OUT) if again else []),
        out_specs=(HB,) * len(MLP_OUT),
        scratch_shapes=[pltpu.VMEM(o.shape, o.dtype) for o in MLP_HELD]
        + [
            pltpu.VMEM(up_w.shape, BF),
            pltpu.VMEM(down_w.shape, BF),
            pltpu.VMEM(slope.shape, BF),
            pltpu.VMEM(two.shape, F32),
            pltpu.VMEM((ROWS, WIDTH), F32),
            pltpu.SemaphoreType.DMA((3 * (FF // TILE) + 1,)),
            pltpu.SemaphoreType.DMA((len(MLP_OUT),)),
        ],
        input_output_aliases={len(given) + i: i for i in range(len(MLP_OUT))} if again else {},
        compiler_params=pltpu.CompilerParams(vmem_limit_bytes=BIG),
        cost_estimate=pl.CostEstimate(flops=5 * 10**9, bytes_accessed=25 * 10**6, transcendentals=0),
    )(*given, *(earlier if again else ()))


ATTEND_OUT = (
    (
        shape((ROWS, WIDTH), F32),
        shape((8, WIDTH), F32),
    )
    + (shape((ROWS, WIDTH), BF),) * SIDE
)
ATTEND_HELD = ATTEND_OUT[:2] + (shape((SIDE, ROWS, WIDTH), BF),)


def attend_back_kernel(again, after, through, *refs):
    active, order, grad_two, qkv_hbm, lse, seg_c, seg_r, stream_hbm, gain_one, in_hbm, out_hbm = (
        refs[:11]
    )
    n = len(ATTEND_OUT)
    refs = refs[11 + after + through + (n if again else 0) :]
    outs = refs[:n]
    refs = refs[n + through :]
    held = refs[:3]
    proj_in, proj_out, qkv, stream, mask, given, w_sem, o_sem = refs[3:]
    stream_o, line_o, qkv_o = held

    @pl.when(active[0] == 1)
    def _():
        out_copy = pltpu.make_async_copy(out_hbm, proj_out, w_sem.at[0])
        in_copy = pltpu.make_async_copy(in_hbm, proj_in, w_sem.at[1])
        qkv_copy = pltpu.make_async_copy(qkv_hbm, qkv, w_sem.at[2])
        stream_copy = pltpu.make_async_copy(stream_hbm, stream, w_sem.at[3])
        for copy in (out_copy, qkv_copy, in_copy, stream_copy):
            copy.start()

        def put(i):
            source = held[i] if i < 2 else qkv_o.at[order[8 + i - 2]]
            return pltpu.make_async_copy(source, outs[i], o_sem.at[i])

        mask[...] = jnp.where(seg_c[...] == seg_r[...], 1.0, 0.0)
        halfs = halves()
        lane = lax.broadcasted_iota(jnp.int32, (ROWS, PAIR), 1)
        out_copy.wait()
        given[...] = dot(grad_two[...].astype(BF), proj_out[...], NT).astype(BF)
        qkv_copy.wait()
        per = 3 * WIDTH // SIDE // PAIR

        def attend(i, c):
            q = qkv[:, span(i, PAIR)]
            k = qkv[:, span(PAIRS + i, PAIR)]
            v = qkv[:, span(2 * PAIRS + i, PAIR)]
            g = given[:, span(i, PAIR)]
            dq, dk, dv = [], [], []
            for half in (0, 1):
                raw = dot(q * halfs[half], k, NT) * 0.125
                score = jnp.where(mask[...] > 0.5, raw, MASK_FILL)
                prob = jnp.exp(score - column(lse[...], 2 * i + half))
                grad_prob = dot(g * halfs[half], v, NT)
                inner = jnp.sum(grad_prob * prob, axis=-1, keepdims=True)
                grad_score = (prob * (grad_prob - inner)).astype(BF)
                dq.append(dot(grad_score, k, NN))
                dk.append(dot(grad_score, q, TN))
                dv.append(dot(prob.astype(BF), g, TN))
            for j, (got, scale) in enumerate(((dq, 0.125), (dk, 0.125), (dv, 1.0))):
                block = j * PAIRS + i
                qkv_o[block // per, :, span(block % per, PAIR)] = (
                    jnp.where(lane < HEAD, got[0], got[1]) * scale
                ).astype(BF)
            return c

        lax.fori_loop(0, PAIRS, attend, 0, unroll=4)
        in_copy.wait()
        stream_copy.wait()
        part = 3 * WIDTH // SIDE
        back = dot(qkv_o[0, :, :part], proj_in[:, :part], NT)
        for q in range(1, SIDE):
            back = back + dot(qkv_o[q, :, :part], proj_in[:, q * part : (q + 1) * part], NT)
        normed, factor = normalize(stream[...])
        line_o[...] = jnp.broadcast_to(jnp.sum(back * normed, axis=0, keepdims=True), line_o.shape)
        back = grad_two[...] + norm_back(back * gain_one[...].astype(F32), normed, factor)
        stream_o[...] = back
        last = WIDTH // SIDE
        for q in range(SIDE):
            qkv_o[q, :, part:] = back[:, q * last : (q + 1) * last].astype(BF)
        for i in (2, 3, 4, 5, 0, 1):
            put(i).start()
        for i in range(n):
            put(i).wait()


def attend_back(active, order, grad_two, kept, gain_one, proj_in, proj_out, after, earlier, through):
    again = earlier is not None
    given = (active, order, grad_two, *kept, gain_one, proj_in, proj_out, *after)
    n = len(ATTEND_OUT)
    aliases = {len(given) + i: n + i for i in range(len(through))}
    if again:
        aliases |= {len(given) + len(through) + i: i for i in range(n)}
    found = pl.pallas_call(
        partial(attend_back_kernel, again, len(after), len(through)),
        out_shape=ATTEND_OUT + tuple(shape(t.shape, t.dtype) for t in through),
        in_specs=[SM] * 2
        + [VM, HB, VM, VM, VM, HB, VM]
        + [HB] * (2 + len(after) + len(through))
        + ([HB] * n if again else []),
        out_specs=(HB,) * (n + len(through)),
        scratch_shapes=[pltpu.VMEM(o.shape, o.dtype) for o in ATTEND_HELD]
        + [
            pltpu.VMEM(proj_in.shape, BF),
            pltpu.VMEM(proj_out.shape, BF),
            pltpu.VMEM(kept[0].shape, BF),
            pltpu.VMEM(kept[4].shape, F32),
            pltpu.VMEM((ROWS, ROWS), F32),
            pltpu.VMEM((ROWS, WIDTH), BF),
            pltpu.SemaphoreType.DMA((4,)),
            pltpu.SemaphoreType.DMA((n,)),
        ],
        input_output_aliases=aliases,
        compiler_params=pltpu.CompilerParams(vmem_limit_bytes=BIG),
        cost_estimate=pl.CostEstimate(flops=5 * 10**9, bytes_accessed=15 * 10**6, transcendentals=0),
    )(*given, *through, *(earlier if again else ()))
    return found[:n], found[n:]


def gate_kernel(first, passed, top_grad, *refs):
    refs[-1][...] = jnp.where(first[0] == 1, passed[...].astype(F32), top_grad[...].astype(F32)).astype(BF)


def gate(first, passed, top_grad, after):
    return pl.pallas_call(
        gate_kernel,
        out_shape=shape(passed.shape, BF),
        in_specs=[SM, VM, VM] + [HB] * len(after),
        out_specs=VM,
    )(first, passed, top_grad, *after)


TERMS = WIDTH + KEYS + HEADS


def pool_back_kernel(
    after,
    grad,
    pool_w,
    patch,
    prob,
    value_t,
    table_hbm,
    value_hbm,
    key_hbm,
    probe,
    *refs,
):
    out, line, mixed_t, blend, values, scores, table, value_w, key_w, sem = refs[after:]
    copies = [
        pltpu.make_async_copy(source, target, sem.at[i])
        for i, (source, target) in enumerate(
            ((table_hbm, table), (value_hbm, value_w), (key_hbm, key_w))
        )
    ]
    for copy in copies:
        copy.start()
    mixed_t[...] = dot(pool_w[...], grad[...].astype(BF), NT).astype(BF)
    lane = lax.broadcasted_iota(jnp.int32, (VARS, HEADS), 1)

    def head(h, c):
        rows = span(h, HEAD)
        back = dot(value_t[rows, :], mixed_t[rows, :], TN)
        grad_prob = back[PIX * VARS :]
        for p in range(PIX):
            grad_prob = grad_prob + back[p * VARS : (p + 1) * VARS] * patch[p]
        weight = prob[h]
        inner = jnp.sum(grad_prob * weight, axis=0, keepdims=True)
        grad_score = (weight * (grad_prob - inner)).astype(BF).astype(F32)
        for p in range(PIX + 1):
            lines = slice(p * VARS, (p + 1) * VARS)
            seen = grad_score if p == PIX else grad_score * patch[p]
            total = jnp.sum(seen, axis=-1, keepdims=True) * 0.125
            scores[lines] = jnp.where(lane == h, total, scores[lines])
            blend[lines] = (weight if p == PIX else weight * patch[p]).astype(BF)
        values[rows, :] = dot(mixed_t[rows, :], blend[...], NT).astype(BF)
        return c

    scores[...] = jnp.zeros_like(scores)
    lax.fori_loop(0, HEADS, head, 0, unroll=8)
    score = scores[...].astype(BF)
    for copy in copies:
        copy.wait()
    out[:, :WIDTH] = dot(table[...], values[...], ((0,), (1,))).astype(BF)
    embed = dot(value_w[...], values[...], NN) + dot(probe[...].astype(BF), score, ((0,), (1,)))
    probe_term = dot(table[...], score, TN)
    out[:, WIDTH:] = jnp.concatenate([embed, probe_term], axis=1).astype(BF)
    crossed = dot(probe_term.astype(BF), key_w[...], TN)
    row = lax.broadcasted_iota(jnp.int32, (HEADS, WIDTH), 0)
    col = lax.broadcasted_iota(jnp.int32, (HEADS, WIDTH), 1)
    line[...] = jnp.sum(jnp.where(col // HEAD == row, crossed, 0.0), axis=0, keepdims=True)


def pool_back(grad, pool_w, patch, prob, value_t, table, value_w, key_w, probe, after):
    return pl.pallas_call(
        partial(pool_back_kernel, len(after)),
        out_shape=(shape((WIDTH, TERMS), BF), shape((1, WIDTH), F32)),
        in_specs=[VM] * 5 + [HB] * 3 + [VM] + [HB] * len(after),
        out_specs=(VM, VM),
        scratch_shapes=[
            pltpu.VMEM((WIDTH, ROWS), BF),
            pltpu.VMEM((KEYS, ROWS), BF),
            pltpu.VMEM((WIDTH, KEYS), BF),
            pltpu.VMEM((KEYS, HEADS), F32),
            pltpu.VMEM(table.shape, BF),
            pltpu.VMEM(value_w.shape, BF),
            pltpu.VMEM(key_w.shape, BF),
            pltpu.SemaphoreType.DMA((3,)),
        ],
        compiler_params=pltpu.CompilerParams(vmem_limit_bytes=BIG),
        cost_estimate=pl.CostEstimate(flops=3 * 10**9, bytes_accessed=12 * 10**6, transcendentals=0),
    )(grad, pool_w, patch, prob, value_t, table, value_w, key_w, probe, *after)


def scatter_rows(stage, slots, block, value, axis):
    if axis == 2:
        stage[slots[block]] = value
    elif axis == 1:
        for y in range(SIDE):
            stage[slots[y], pl.ds(block * 64, 64), :] = value[y * 64 : (y + 1) * 64]
    else:
        for y in range(SIDE):
            for x in range(SIDE):
                at = y * 64 + x * 16
                stage[slots[x], pl.ds(block * 64 + y * 16, 16), :] = value[at : at + 16]


def term_kernel(count, offsets, axis, extra, tail, after, slots, *refs):
    left = refs[:count]
    right = [refs[count * (i + 1) : count * (i + 2)] for i in range(len(offsets))]
    refs = refs[count * (len(offsets) + 1) :]
    if extra:
        more, refs = refs[0], refs[1:]
    if tail:
        small, refs = refs[0], refs[1:]
    refs = refs[after:]
    outs, (stage, sem) = refs[:SIDE], refs[SIDE:]
    own = [slots[axis * SIDE + i] for i in range(SIDE)]
    for block in range(SIDE):
        made = []
        for parts, (base, first, size) in zip(right, offsets):
            total = None
            for a, b in zip(left, parts):
                got = dot(
                    a[:, base + block * 256 : base + (block + 1) * 256],
                    b[:, first : first + size],
                    TN,
                )
                total = got if total is None else total + got
            made.append(total.astype(BF))
        if extra:
            made.append(more[block * 256 : (block + 1) * 256, extra[0] : extra[1]])
        made = made[0] if len(made) == 1 else jnp.concatenate(made, axis=1)
        scatter_rows(stage, own, block, made, axis)
    if tail:
        for k in range(SIDE):
            stage[k, WIDTH // SIDE :, :WIDTH] = small[...]
            stage[k, WIDTH // SIDE :, WIDTH:] = jnp.zeros((tail, stage.shape[2] - WIDTH), BF)
    copies = [pltpu.make_async_copy(stage.at[k], outs[k], sem.at[k]) for k in range(SIDE)]
    for c in copies:
        c.start()
    for c in copies:
        c.wait()


def weight_term(
    slots, left, rights, offsets, axis, extra=None, more=None, small=None, after=()
):
    columns = sum(o[2] for o in offsets) + (extra[1] - extra[0] if extra else 0)
    tail = 0 if small is None else small.shape[0]
    out = shape((WIDTH // SIDE + tail, columns), BF)
    given = [*left, *[r for parts in rights for r in parts]]
    given += [more] if extra else []
    given += [small] if tail else []
    return pl.pallas_call(
        partial(term_kernel, len(left), offsets, axis, extra, tail, len(after)),
        out_shape=(out,) * SIDE,
        in_specs=[SM] + [VM] * len(given) + [HB] * len(after),
        out_specs=(HB,) * SIDE,
        scratch_shapes=[pltpu.VMEM((SIDE,) + out.shape, BF), pltpu.SemaphoreType.DMA((SIDE,))],
        compiler_params=pltpu.CompilerParams(vmem_limit_bytes=BIG),
        cost_estimate=pl.CostEstimate(flops=2 * 10**9, bytes_accessed=5 * 10**6, transcendentals=0),
    )(slots, *given, *after)


def add_kernel(axis, inner, tail, slots, a, b, c, d, *refs):
    outs, (stage, sem) = refs[:SIDE], refs[SIDE:]
    rows = a.shape[0] - tail
    part = rows // SIDE
    total = a[...].astype(F32) + b[...].astype(F32) + c[...].astype(F32) + d[...].astype(F32)
    total = total.astype(BF)
    for i in range(SIDE):
        slot = slots[axis * SIDE + i]
        if inner:
            for j in range(SIDE):
                at = (j * SIDE + i) * 16
                stage[slot, j * 16 : (j + 1) * 16, :] = total[at : at + 16]
        else:
            stage[slot, :part, :] = total[i * part : (i + 1) * part]
        if tail:
            stage[slot, part:, :] = total[rows:]
    copies = [pltpu.make_async_copy(stage.at[k], outs[k], sem.at[k]) for k in range(SIDE)]
    for c in copies:
        c.start()
    for c in copies:
        c.wait()


def add_up(slots, pieces, axis, inner, tail=0):
    rows, columns = pieces[0].shape
    out = shape(((rows - tail) // SIDE + tail, columns), BF)
    return pl.pallas_call(
        partial(add_kernel, axis, inner, tail),
        out_shape=(out,) * SIDE,
        in_specs=[SM] + [VM] * 4,
        out_specs=(HB,) * SIDE,
        scratch_shapes=[pltpu.VMEM((SIDE,) + out.shape, BF), pltpu.SemaphoreType.DMA((SIDE,))],
        compiler_params=pltpu.CompilerParams(vmem_limit_bytes=BIG),
        cost_estimate=pl.CostEstimate(flops=10**6, bytes_accessed=5 * 10**6, transcendentals=0),
    )(slots, *pieces)


def last_kernel(order, *refs):
    xs, ys, zs = refs[:4], refs[4:8], refs[8:12]
    query_vec, var_q, query_w = refs[12:15]
    (
        up,
        out,
        down,
        into,
        pool,
        value,
        embed,
        var,
        key,
        qweight,
        vquery,
        line_two,
        line_down,
        line_one,
        line_up,
    ) = refs[15:]
    wide, narrow, third = FF // SIDE, WIDTH // SIDE, 3 * WIDTH // SIDE
    own = up.shape[0]
    total_x = total_y = small = 0.0
    for k in range(SIDE):
        back = (SIDE - k) % SIDE
        q = order[back]
        up[:, span(q, wide)] = xs[k][:own, :wide].astype(F32)
        out[:, span(q, narrow)] = xs[k][:own, wide : wide + narrow].astype(F32)
        q = order[4 + back]
        down[:, span(q, wide)] = ys[k][:, :wide].astype(F32)
        q = order[8 + back]
        into[:, span(q, third)] = zs[k][:, :third].astype(F32)
        pool[:, span(q, narrow)] = zs[k][:, third:].astype(F32)
        total_x = total_x + xs[k][:own, wide + narrow :].astype(F32)
        total_y = total_y + ys[k][:, wide:].astype(F32)
        small = small + xs[k][own:, :WIDTH].astype(F32)
    total = jnp.concatenate([total_y, total_x], axis=1)
    value[...] = total[:, :WIDTH]
    for p in range(PIX):
        at = WIDTH + p * VARS
        embed[p] = total[:, at : at + VARS]
    var[...] = total[:, WIDTH + PIX * VARS : WIDTH + KEYS]
    row = lax.broadcasted_iota(jnp.int32, (HEADS, WIDTH), 0)
    col = lax.broadcasted_iota(jnp.int32, (HEADS, WIDTH), 1)
    spread = jnp.where(col // HEAD == row, 1.0, 0.0)
    probe = jnp.dot(
        total[:, WIDTH + KEYS :],
        spread,
        precision=lax.Precision.HIGHEST,
        preferred_element_type=F32,
    )
    key[...] = probe * query_vec[...]
    qvec = small[0:1]
    qweight[...] = var_q[...] * qvec
    exact = partial(
        lax.dot_general, precision=lax.Precision.HIGHEST, preferred_element_type=F32
    )
    vquery[...] = exact(qvec, query_w[...].astype(F32), (NT, ((), ())))
    chip = order[8] * SIDE * SIDE + order[4] * SIDE + order[0]
    row = lax.broadcasted_iota(jnp.int32, (WIDTH, own), 0)
    col = lax.broadcasted_iota(jnp.int32, (WIDTH, own), 1)
    mine = exact(small, jnp.where(row == chip * own + col, 1.0, 0.0), (NN, ((), ())))
    line_two[...] = mine[1:2]
    line_down[...] = mine[2:3]
    line_one[...] = mine[7:8]
    row = lax.broadcasted_iota(jnp.int32, (WIDTH, SIDE * own), 0)
    col = lax.broadcasted_iota(jnp.int32, (WIDTH, SIDE * own), 1)
    first = (chip % (SIDE * SIDE)) * SIDE * own
    mine = exact(small, jnp.where(row == first + col, 1.0, 0.0), (NN, ((), ())))
    row = lax.broadcasted_iota(jnp.int32, mine.shape, 0)
    line_up[...] = jnp.sum(
        jnp.where(row == 3 + order[8], mine, 0.0), axis=0, keepdims=True
    )


def last_step(order, xs, ys, zs, query_vec, var_q, query_w):
    own = WIDTH // SIDE**3
    return pl.pallas_call(
        last_kernel,
        out_shape=(
            shape((own, FF), F32),
            shape((own, WIDTH), F32),
            shape((own, FF), F32),
            shape((own, 3 * WIDTH), F32),
            shape((own, WIDTH), F32),
            shape((own, WIDTH), F32),
            shape((PIX, own, VARS), F32),
            shape((own, VARS), F32),
            shape((own, WIDTH), F32),
            shape((own, WIDTH), F32),
            shape((1, own), F32),
            shape((1, own), F32),
            shape((1, own), F32),
            shape((1, own), F32),
            shape((1, SIDE * own), F32),
        ),
        in_specs=[SM] + [VM] * 15,
        out_specs=(VM,) * 15,
        compiler_params=pltpu.CompilerParams(vmem_limit_bytes=BIG),
    )(order, *xs, *ys, *zs, query_vec, var_q, query_w)


def local(
    tokens,
    pixels,
    segments,
    embed_weight,
    var_embed,
    var_query,
    query_weight,
    key_weight,
    value_weight,
    pool_weight,
    first_gain,
    project_in,
    project_out,
    second_gain,
    up_weight,
    up_bias,
    down_weight,
    down_bias,
    cotangent,
):
    section = lax.axis_index("section")
    is_first = section == 0
    micro, _, seq, width = tokens.shape
    rows = micro * seq
    value_w, query_w, key_w = value_weight[0], query_weight[0], key_weight[0]
    up_w, down_w, proj_in, proj_out, pool_w = (
        w[0] for w in (up_weight, down_weight, project_in, project_out, pool_weight)
    )
    table = jnp.concatenate(
        [embed_weight[0].transpose(1, 0, 2).reshape(PIX * VARS, width), var_embed[0]]
    )
    query_vec, probe, quick, value_t = prepare(table, var_query, query_w, key_w, value_w)
    patch = pixels[:, 0].astype(F32).transpose(2, 1, 0, 3).reshape(PIX, VARS, rows)
    seg_ids = (segments[:, 0] + SIDE * jnp.arange(micro)[:, None]).reshape(rows)
    seg_c, seg_r = seg_ids[:, None], seg_ids[None]
    inputs = tokens.reshape(rows, width)
    on_first = jnp.where(is_first, 1, 0).astype(jnp.int32).reshape(1)
    on_second = 1 - on_first

    sign = jnp.where(is_first, 1, -1)
    steps = jnp.arange(SIDE)
    spots = [place(axis) for axis in "xyz"]
    order = jnp.concatenate([(at + sign * steps) % SIDE for at in spots]).astype(jnp.int32)
    slots = jnp.concatenate([(sign * (steps - at)) % SIDE for at in spots]).astype(jnp.int32)

    base = (patch, seg_c, seg_r, quick, value_t)
    lines = (first_gain, second_gain, up_bias, down_bias)
    weights = (pool_w, proj_in, proj_out, up_w, down_w)
    saved = forward(on_first, order, inputs, base, lines, weights, None)
    passed = lax.ppermute(saved[0], "section", [(0, 1)])
    saved = forward(on_second, order, passed, base, lines, weights, saved)
    result, prob, stream, stream_two, qkv, lse, slope, for_x, for_z = saved[:9]
    hidden = saved[9:]
    kept = (qkv, lse, seg_c, seg_r, stream)

    top_grad = cotangent.reshape(rows, width)
    low = mlp_back(
        on_second, order, top_grad, stream_two, slope, second_gain, up_w, down_w, (), None
    )
    all_x = share(for_x, "x")
    first_z = [swap(for_z, "z", k) for k in (1, 3)]
    high, (for_z, *hidden) = attend_back(
        on_second,
        order,
        low[0],
        kept,
        first_gain,
        proj_in,
        proj_out,
        (*all_x[1:], *first_z),
        None,
        (for_z, *hidden),
    )
    passed = lax.ppermute(high[0].astype(BF), "section", [(1, 0)])
    all_z = [for_z, first_z[0], swap(for_z, "z", 2), first_z[1]]
    all_y = handed(hidden, "y")
    branch_down = gate(on_first, passed, top_grad, (*all_y[1:], all_z[2]))
    down_all = share(branch_down, "y")
    low = mlp_back(
        on_first, order, branch_down, stream_two, slope, second_gain, up_w, down_w, (), low
    )
    high, _ = attend_back(
        on_first, order, low[0], kept, first_gain, proj_in, proj_out, tuple(down_all[1:]), high, ()
    )
    low_lines, grad_pre = low[1], low[2:]
    grad_in, high_lines, grad_qkv = high[0], high[1], high[2:]

    pre_all = handed(grad_pre, "x")
    qkv_all = handed(grad_qkv, "z")
    more, qvec_term = pool_back(
        grad_in, pool_w, patch, prob, value_t, table, value_w, key_w, probe, ()
    )
    small = jnp.concatenate(
        [qvec_term, low_lines[:6], high_lines[:1], jnp.zeros((8, width), F32)]
    ).astype(BF)

    wide, narrow, third = FF // SIDE, WIDTH // SIDE, 3 * WIDTH // SIDE
    half = TERMS // 2
    ys = weight_term(
        slots, down_all, [all_y], ((0, 0, wide),), 2, (0, half), more
    )
    xs = weight_term(
        slots,
        all_x,
        [pre_all, pre_all],
        ((0, 0, wide), (WIDTH, wide, narrow)),
        1,
        (half, TERMS),
        more,
        small,
    )
    zs = weight_term(
        slots,
        all_z,
        [qkv_all, qkv_all],
        ((0, 0, third), (WIDTH, third, narrow)),
        0,
    )
    tail = small.shape[0]
    ys = add_up(slots, handed(ys, "z"), 0, True)
    xs = add_up(slots, handed(xs, "y"), 2, False, tail)
    zs = add_up(slots, handed(zs, "x"), 1, True)
    ys = add_up(slots, handed(ys, "x"), 1, False)
    xs = add_up(slots, handed(xs, "z"), 0, False, tail)
    zs = add_up(slots, handed(zs, "y"), 2, False)
    own = width // SIDE**3
    at = lax.axis_index("batch") * own
    mine = partial(lax.dynamic_slice_in_dim, start_index=at, slice_size=own)
    (
        grad_up,
        grad_out,
        grad_down,
        grad_in_w,
        grad_pool,
        grad_value,
        grad_embed,
        grad_var,
        grad_key,
        grad_qw,
        grad_vq,
        line_two,
        line_down,
        line_one,
        line_up,
    ) = last_step(
        order,
        handed(xs, "x"),
        handed(ys, "y"),
        handed(zs, "z"),
        query_vec,
        mine(var_query[0], axis=0).astype(F32)[:, None],
        mine(query_w, axis=0),
    )
    grad_embed = grad_embed.transpose(2, 0, 1)
    grad_var = grad_var.T
    grad_down = grad_down.T

    return (
        result.reshape(1, micro, 1, seq, width),
        grad_in.reshape(1, micro, 1, seq, width),
        grad_embed[None],
        grad_var[None],
        grad_vq,
        grad_qw[None],
        grad_key[None],
        grad_value[None],
        grad_pool[None],
        line_one,
        grad_in_w[None],
        grad_out[None],
        line_two,
        grad_up[None],
        line_up,
        grad_down[None],
        line_down,
    )


def solution(mesh):
    in_specs = (
        P(None, "batch", None, None),
        P(None, "batch", None, None, None),
        P(None, "batch", None),
        P("section", None, None, None),
        P("section", None, None),
        P("section", None),
        P("section", None, None),
        P("section", None, None),
        P("section", None, None),
        P("section", None, None),
        P("section", None),
        P("section", None, None),
        P("section", None, None),
        P("section", None),
        P("section", None, None),
        P("section", None),
        P("section", None, None),
        P("section", None),
        P(None, "batch", None, None),
    )
    out_specs = (
        P("section", None, "batch", None, None),
        P("section", None, "batch", None, None),
        P("section", None, None, "batch"),
        P("section", None, "batch"),
        P("section", "batch"),
        P("section", "batch", None),
        P("section", "batch", None),
        P("section", "batch", None),
        P("section", "batch", None),
        P("section", "batch"),
        P("section", "batch", None),
        P("section", "batch", None),
        P("section", "batch"),
        P("section", "batch", None),
        P("section", "batch"),
        P("section", None, "batch"),
        P("section", "batch"),
    )
    return jax.shard_map(local, mesh=mesh, in_specs=in_specs, out_specs=out_specs, check_vma=False)
```

```python
from functools import partial

import jax
import jax.numpy as jnp
from jax import lax
from jax.experimental import pallas as pl
from jax.experimental.pallas import tpu as pltpu
from jax.sharding import PartitionSpec as P

HEADS = 16
HEAD = 64
VARS = 48
PIX = 4
SIDE = 4
MASK_FILL = -1000000000.0
NORM_EPS = 1e-06
STRIDE = {"x": 1, "y": SIDE, "z": SIDE * SIDE}
BF = jnp.bfloat16
F32 = jnp.float32


def dot(a, b, contract):
    return lax.dot_general(a, b, (contract, ((), ())), preferred_element_type=F32)


def moved(axis, step):
    chips = SIDE**3
    pairs = []
    for section in (0, 1):
        signed = step if section == 0 else -step
        for chip in range(chips):
            at = (chip // STRIDE[axis]) % SIDE
            to = chip + ((at + signed) % SIDE - at) * STRIDE[axis]
            pairs.append((section * chips + chip, section * chips + to))
    return pairs


def swap(value, axis, step):
    return lax.ppermute(value, ("section", "batch"), moved(axis, step))


def place(axis):
    return (lax.axis_index("batch") // STRIDE[axis]) % SIDE


def share(value, axis):
    return [value] + [swap(value, axis, k) for k in (1, 2, 3)]


def handed(parts, axis):
    return [parts[0]] + [swap(parts[k], axis, k) for k in (1, 2, 3)]


VM = pl.BlockSpec(memory_space=pltpu.VMEM)
SM = pl.BlockSpec(memory_space=pltpu.SMEM)
HB = pl.BlockSpec(memory_space=pl.ANY)
BIG = 60 * 1024 * 1024
ROWS = 256
WIDTH = HEADS * HEAD
FF = 4096
TILE = 1024
KEYS = (PIX + 1) * VARS
PAIR = 2 * HEAD
PAIRS = HEADS // 2
NN = ((1,), (0,))
NT = ((1,), (1,))
TN = ((0,), (0,))


def span(index, size):
    return pl.ds(pl.multiple_of(index * size, size), size)


def shape(dims, dtype):
    return jax.ShapeDtypeStruct(dims, dtype)


def prepare_kernel(
    table, var_q, query_hbm, key_hbm, value_hbm, query_vec, probe, quick, value_t, query_w, key_w, value_w, sem
):
    copies = [
        pltpu.make_async_copy(source, target, sem.at[i])
        for i, (source, target) in enumerate(
            ((value_hbm, value_w), (query_hbm, query_w), (key_hbm, key_w))
        )
    ]
    for copy in copies:
        copy.start()
    copies[0].wait()
    value_t[...] = dot(table[...], value_w[...], NN).T.astype(BF)
    copies[1].wait()
    found = dot(jnp.broadcast_to(var_q[...], (16, WIDTH)), query_w[...], NN).astype(BF)
    query_vec[...] = found[0:1].astype(F32)
    head = lax.broadcasted_iota(jnp.int32, (16, WIDTH), 0)
    lane = lax.broadcasted_iota(jnp.int32, (16, WIDTH), 1)
    spread = jnp.where(lane // HEAD == head, found.astype(F32), 0.0).astype(BF)
    copies[2].wait()
    made = dot(spread, key_w[...], NT).astype(BF)
    probe[...] = made.astype(F32)
    quick[...] = dot(table[...], made, NT) * 0.125


def prepare(table, var_q, query_w, key_w, value_w):
    return pl.pallas_call(
        prepare_kernel,
        out_shape=(
            shape((1, WIDTH), F32),
            shape((HEADS, WIDTH), F32),
            shape((KEYS, HEADS), F32),
            shape((WIDTH, KEYS), BF),
        ),
        in_specs=[VM] * 2 + [HB] * 3,
        out_specs=(VM,) * 4,
        scratch_shapes=[pltpu.VMEM(w.shape, BF) for w in (query_w, key_w, value_w)]
        + [pltpu.SemaphoreType.DMA((3,))],
        compiler_params=pltpu.CompilerParams(vmem_limit_bytes=BIG),
    )(table, var_q, query_w, key_w, value_w)


def normalize(value):
    center = value - jnp.mean(value, axis=-1, keepdims=True)
    factor = lax.rsqrt(jnp.mean(center * center, axis=-1, keepdims=True) + NORM_EPS)
    return (center * factor, factor)


def norm_back(grad, normed, factor):
    return factor * (
        grad
        - jnp.mean(grad, axis=-1, keepdims=True)
        - normed * jnp.mean(grad * normed, axis=-1, keepdims=True)
    )


def halves():
    lane = lax.broadcasted_iota(jnp.int32, (1, PAIR), 1)
    return [jnp.where(lane // HEAD == half, 1.0, 0.0).astype(BF) for half in (0, 1)]


def column(value, index):
    lane = lax.broadcasted_iota(jnp.int32, value.shape, 1)
    return jnp.sum(jnp.where(lane == index, value, 0.0), axis=-1, keepdims=True)


FORWARD_OUT = (
    shape((ROWS, WIDTH), BF),
    shape((HEADS, VARS, ROWS), F32),
    shape((ROWS, WIDTH), F32),
    shape((ROWS, WIDTH), F32),
    shape((ROWS, 3 * WIDTH), BF),
    shape((ROWS, 128), F32),
    shape((ROWS, FF), BF),
    shape((ROWS, 2 * WIDTH), BF),
    shape((ROWS, 2 * WIDTH), BF),
) + (shape((ROWS, FF // SIDE), BF),) * SIDE
FORWARD_HELD = FORWARD_OUT[:9] + (shape((SIDE, ROWS, FF // SIDE), BF),)


def forward_kernel(again, *refs):
    active, order = refs[:2]
    (inputs, patch, seg_c, seg_r, quick, value_t, gain_one, gain_two, up_b, down_b) = refs[2:12]
    weights = refs[12:17]
    refs = refs[17:]
    n = len(FORWARD_OUT)
    if again:
        refs = refs[n:]
    outs, held = refs[:n], refs[n : n + len(FORWARD_HELD)]
    refs = refs[n + len(FORWARD_HELD) :]
    pool_w, proj_in, proj_out, up_w, down_w = refs[:5]
    blend, mask, acc, w_sem, o_sem = refs[5:]
    result, prob_o, stream_o, two_o, qkv_o, lse_o, slope_o, for_x, for_z, for_y = held

    @pl.when(active[0] == 1)
    def _():
        def fetch(i):
            return pltpu.make_async_copy(
                weights[i], (pool_w, proj_in, proj_out, up_w, down_w)[i], w_sem.at[i]
            )

        def put(i):
            source = held[i] if i < 9 else for_y.at[order[4 + i - 9]]
            return pltpu.make_async_copy(source, outs[i], o_sem.at[i])

        for i in range(5):
            fetch(i).start()
        for pair in range(PAIRS):
            both = []
            for head in (2 * pair, 2 * pair + 1):
                score = quick[PIX * VARS :, head : head + 1] + jnp.zeros((VARS, ROWS), F32)
                for p in range(PIX):
                    score = score + quick[p * VARS : (p + 1) * VARS, head : head + 1] * patch[p]
                grown = jnp.exp(score - jnp.max(score, axis=0, keepdims=True))
                prob = grown / jnp.sum(grown, axis=0, keepdims=True)
                prob_o[head] = prob
                for p in range(PIX):
                    blend[p * VARS : (p + 1) * VARS] = (prob * patch[p]).astype(BF)
                blend[PIX * VARS :] = prob.astype(BF)
                both.append(dot(value_t[head * HEAD : (head + 1) * HEAD], blend[...], NN))
            at = WIDTH + pair * PAIR
            for_z[:, at : at + PAIR] = jnp.concatenate(both, axis=0).T.astype(BF)
        put(1).start()
        fetch(0).wait()
        stream = inputs[...].astype(F32) + dot(for_z[:, WIDTH:], pool_w[...], NN)
        stream_o[...] = stream
        put(2).start()
        normed, _ = normalize(stream)
        for_z[:, :WIDTH] = (normed * gain_one[...].astype(F32)).astype(BF)
        put(8).start()
        fetch(1).wait()

        def project(i, c):
            qkv_o[:, span(i, TILE)] = dot(for_z[:, :WIDTH], proj_in[:, span(i, TILE)], NN).astype(BF)
            return c

        lax.fori_loop(0, 3 * WIDTH // TILE, project, 0)
        put(4).start()
        mask[...] = jnp.where(seg_c[...] == seg_r[...], 1.0, 0.0)
        halfs = halves()
        lane = lax.broadcasted_iota(jnp.int32, (ROWS, 128), 1)

        def attend(i, lse):
            q = qkv_o[:, span(i, PAIR)]
            k = qkv_o[:, span(PAIRS + i, PAIR)]
            v = qkv_o[:, span(2 * PAIRS + i, PAIR)]
            got = []
            for half in (0, 1):
                raw = dot(q * halfs[half], k, NT) * 0.125
                score = jnp.where(mask[...] > 0.5, raw, MASK_FILL)
                top = jnp.max(score, axis=-1, keepdims=True)
                grown = jnp.exp(score - top)
                total = jnp.sum(grown, axis=-1, keepdims=True)
                lse = jnp.where(lane == 2 * i + half, top + jnp.log(total), lse)
                got.append(dot((grown / total).astype(BF), v, NN))
            for_x[:, span(PAIRS + i, PAIR)] = jnp.where(lane < HEAD, got[0], got[1]).astype(BF)
            return lse

        lse_o[...] = lax.fori_loop(0, PAIRS, attend, jnp.zeros((ROWS, 128), F32), unroll=True)
        put(5).start()
        fetch(2).wait()
        two = stream_o[...] + dot(for_x[:, WIDTH:], proj_out[...], NN)
        two_o[...] = two
        put(3).start()
        normed, _ = normalize(two)
        for_x[:, :WIDTH] = (normed * gain_two[...].astype(F32)).astype(BF)
        put(7).start()
        acc[...] = two + down_b[...].astype(F32)
        fetch(3).wait()
        fetch(4).wait()

        def mlp(i, c):
            pre = dot(for_x[:, :WIDTH], up_w[:, span(i, TILE)], NN) + up_b[:, span(i, TILE)].astype(F32)
            cdf = 0.5 * (1.0 + lax.erf(pre * 0.7071067811865476))
            slope_o[:, span(i, TILE)] = (
                cdf + pre * (jnp.exp(-0.5 * pre * pre) * 0.3989422804014327)
            ).astype(BF)
            hid = (pre * cdf).astype(BF)
            per = FF // SIDE // TILE
            for_y[i // per, :, span(i % per, TILE)] = hid
            acc[...] += dot(hid, down_w[span(i, TILE), :], NN)
            return c

        lax.fori_loop(0, FF // TILE, mlp, 0, unroll=True)
        result[...] = acc[...].astype(BF)
        for i in (0, 6, 9, 10, 11, 12):
            put(i).start()
        for i in range(n):
            put(i).wait()


def forward(active, order, inputs, base, lines, weights, earlier):
    again = earlier is not None
    given = (active, order, inputs, *base, *lines, *weights)
    return pl.pallas_call(
        partial(forward_kernel, again),
        out_shape=FORWARD_OUT,
        in_specs=[SM] * 2 + [VM] * 10 + [HB] * 5 + ([HB] * len(FORWARD_OUT) if again else []),
        out_specs=(HB,) * len(FORWARD_OUT),
        scratch_shapes=[pltpu.VMEM(o.shape, o.dtype) for o in FORWARD_HELD]
        + [pltpu.VMEM(w.shape, w.dtype) for w in weights]
        + [
            pltpu.VMEM((KEYS, ROWS), BF),
            pltpu.VMEM((ROWS, ROWS), F32),
            pltpu.VMEM((ROWS, WIDTH), F32),
            pltpu.SemaphoreType.DMA((5,)),
            pltpu.SemaphoreType.DMA((len(FORWARD_OUT),)),
        ],
        input_output_aliases={len(given) + i: i for i in range(len(FORWARD_OUT))} if again else {},
        compiler_params=pltpu.CompilerParams(vmem_limit_bytes=BIG),
        cost_estimate=pl.CostEstimate(flops=8 * 10**9, bytes_accessed=40 * 10**6, transcendentals=0),
    )(*given, *(earlier if again else ()))


MLP_OUT = (
    shape((ROWS, WIDTH), F32),
    shape((8, WIDTH), F32),
) + (shape((ROWS, (FF + WIDTH) // SIDE), BF),) * SIDE
MLP_HELD = MLP_OUT[:2] + (shape((SIDE, ROWS, (FF + WIDTH) // SIDE), BF),)


def mlp_back_kernel(again, after, *refs):
    active, order, grad, two_hbm, slope_hbm, gain_two, up_hbm, down_hbm = refs[:8]
    n = len(MLP_OUT)
    refs = refs[8 + after + (n if again else 0) :]
    outs, held = refs[:n], refs[n : n + 3]
    up_w, down_w, slope, two, acc, w_sem, o_sem = refs[n + 3 :]
    two_o, line_o, pre_o = held
    tiles = FF // TILE

    @pl.when(active[0] == 1)
    def _():
        fetches = []
        for i in range(tiles):
            at = pl.ds(i * TILE, TILE)
            fetches.append(
                [
                    pltpu.make_async_copy(down_hbm.at[at, :], down_w.at[at, :], w_sem.at[3 * i]),
                    pltpu.make_async_copy(slope_hbm.at[:, at], slope.at[:, at], w_sem.at[3 * i + 1]),
                    pltpu.make_async_copy(up_hbm.at[:, at], up_w.at[:, at], w_sem.at[3 * i + 2]),
                ]
            )
        fetch_two = pltpu.make_async_copy(two_hbm, two, w_sem.at[3 * tiles])
        for fetch in fetches:
            for copy in fetch:
                copy.start()
        fetch_two.start()

        def put(i):
            source = held[i] if i < 2 else pre_o.at[order[i - 2]]
            return pltpu.make_async_copy(source, outs[i], o_sem.at[i])

        line_o[...] = jnp.zeros_like(line_o)
        per = FF // SIDE // TILE
        for i in range(tiles):
            for copy in fetches[i]:
                copy.wait()
            at = slice(i * TILE, (i + 1) * TILE)
            inner = slice((i % per) * TILE, (i % per + 1) * TILE)
            hid = dot(grad[...], down_w[at, :], NT).astype(BF).astype(F32)
            pre = (hid * slope[:, at].astype(F32)).astype(BF)
            pre_o[i // per, :, inner] = pre
            line_o[2 + i // per : 3 + i // per, inner] = jnp.sum(
                pre.astype(F32), axis=0, keepdims=True
            )
            got = dot(pre, up_w[:, at], NT)
            acc[...] = got if i == 0 else acc[...] + got
        fetch_two.wait()
        normed, factor = normalize(two[...])
        got = acc[...]
        line_o[0:1] = jnp.sum(got * normed, axis=0, keepdims=True)
        line_o[1:2] = jnp.sum(grad[...].astype(F32), axis=0, keepdims=True)
        back = grad[...].astype(F32) + norm_back(got * gain_two[...].astype(F32), normed, factor)
        two_o[...] = back
        for q in range(SIDE):
            part = WIDTH // SIDE
            pre_o[q, :, FF // SIDE :] = back[:, q * part : (q + 1) * part].astype(BF)
        for i in range(n):
            put(i).start()
        for i in range(n):
            put(i).wait()


def mlp_back(active, order, grad, two, slope, gain_two, up_w, down_w, after, earlier):
    again = earlier is not None
    given = (active, order, grad, two, slope, gain_two, up_w, down_w, *after)
    return pl.pallas_call(
        partial(mlp_back_kernel, again, len(after)),
        out_shape=MLP_OUT,
        in_specs=[SM] * 2
        + [VM, HB, HB, VM]
        + [HB] * (2 + len(after))
        + ([HB] * len(MLP_OUT) if again else []),
        out_specs=(HB,) * len(MLP_OUT),
        scratch_shapes=[pltpu.VMEM(o.shape, o.dtype) for o in MLP_HELD]
        + [
            pltpu.VMEM(up_w.shape, BF),
            pltpu.VMEM(down_w.shape, BF),
            pltpu.VMEM(slope.shape, BF),
            pltpu.VMEM(two.shape, F32),
            pltpu.VMEM((ROWS, WIDTH), F32),
            pltpu.SemaphoreType.DMA((3 * (FF // TILE) + 1,)),
            pltpu.SemaphoreType.DMA((len(MLP_OUT),)),
        ],
        input_output_aliases={len(given) + i: i for i in range(len(MLP_OUT))} if again else {},
        compiler_params=pltpu.CompilerParams(vmem_limit_bytes=BIG),
        cost_estimate=pl.CostEstimate(flops=5 * 10**9, bytes_accessed=25 * 10**6, transcendentals=0),
    )(*given, *(earlier if again else ()))


ATTEND_OUT = (
    (
        shape((ROWS, WIDTH), F32),
        shape((8, WIDTH), F32),
    )
    + (shape((ROWS, WIDTH), BF),) * SIDE
)
ATTEND_HELD = ATTEND_OUT[:2] + (shape((SIDE, ROWS, WIDTH), BF),)


def attend_back_kernel(again, after, through, *refs):
    active, order, grad_two, qkv_hbm, lse, seg_c, seg_r, stream_hbm, gain_one, in_hbm, out_hbm = (
        refs[:11]
    )
    n = len(ATTEND_OUT)
    refs = refs[11 + after + through + (n if again else 0) :]
    outs = refs[:n]
    refs = refs[n + through :]
    held = refs[:3]
    proj_in, proj_out, qkv, stream, mask, given, w_sem, o_sem = refs[3:]
    stream_o, line_o, qkv_o = held

    @pl.when(active[0] == 1)
    def _():
        out_copy = pltpu.make_async_copy(out_hbm, proj_out, w_sem.at[0])
        in_copy = pltpu.make_async_copy(in_hbm, proj_in, w_sem.at[1])
        qkv_copy = pltpu.make_async_copy(qkv_hbm, qkv, w_sem.at[2])
        stream_copy = pltpu.make_async_copy(stream_hbm, stream, w_sem.at[3])
        for copy in (out_copy, qkv_copy, in_copy, stream_copy):
            copy.start()

        def put(i):
            source = held[i] if i < 2 else qkv_o.at[order[8 + i - 2]]
            return pltpu.make_async_copy(source, outs[i], o_sem.at[i])

        mask[...] = jnp.where(seg_c[...] == seg_r[...], 1.0, 0.0)
        halfs = halves()
        lane = lax.broadcasted_iota(jnp.int32, (ROWS, PAIR), 1)
        out_copy.wait()
        given[...] = dot(grad_two[...].astype(BF), proj_out[...], NT).astype(BF)
        qkv_copy.wait()
        per = 3 * WIDTH // SIDE // PAIR

        def attend(i, c):
            q = qkv[:, span(i, PAIR)]
            k = qkv[:, span(PAIRS + i, PAIR)]
            v = qkv[:, span(2 * PAIRS + i, PAIR)]
            g = given[:, span(i, PAIR)]
            dq, dk, dv = [], [], []
            for half in (0, 1):
                raw = dot(q * halfs[half], k, NT) * 0.125
                score = jnp.where(mask[...] > 0.5, raw, MASK_FILL)
                prob = jnp.exp(score - column(lse[...], 2 * i + half))
                grad_prob = dot(g * halfs[half], v, NT)
                inner = jnp.sum(grad_prob * prob, axis=-1, keepdims=True)
                grad_score = (prob * (grad_prob - inner)).astype(BF)
                dq.append(dot(grad_score, k, NN))
                dk.append(dot(grad_score, q, TN))
                dv.append(dot(prob.astype(BF), g, TN))
            for j, (got, scale) in enumerate(((dq, 0.125), (dk, 0.125), (dv, 1.0))):
                block = j * PAIRS + i
                qkv_o[block // per, :, span(block % per, PAIR)] = (
                    jnp.where(lane < HEAD, got[0], got[1]) * scale
                ).astype(BF)
            return c

        lax.fori_loop(0, PAIRS, attend, 0, unroll=4)
        in_copy.wait()
        stream_copy.wait()
        part = 3 * WIDTH // SIDE
        back = dot(qkv_o[0, :, :part], proj_in[:, :part], NT)
        for q in range(1, SIDE):
            back = back + dot(qkv_o[q, :, :part], proj_in[:, q * part : (q + 1) * part], NT)
        normed, factor = normalize(stream[...])
        line_o[...] = jnp.broadcast_to(jnp.sum(back * normed, axis=0, keepdims=True), line_o.shape)
        back = grad_two[...] + norm_back(back * gain_one[...].astype(F32), normed, factor)
        stream_o[...] = back
        last = WIDTH // SIDE
        for q in range(SIDE):
            qkv_o[q, :, part:] = back[:, q * last : (q + 1) * last].astype(BF)
        for i in (2, 3, 4, 5, 0, 1):
            put(i).start()
        for i in range(n):
            put(i).wait()


def attend_back(active, order, grad_two, kept, gain_one, proj_in, proj_out, after, earlier, through):
    again = earlier is not None
    given = (active, order, grad_two, *kept, gain_one, proj_in, proj_out, *after)
    n = len(ATTEND_OUT)
    aliases = {len(given) + i: n + i for i in range(len(through))}
    if again:
        aliases |= {len(given) + len(through) + i: i for i in range(n)}
    found = pl.pallas_call(
        partial(attend_back_kernel, again, len(after), len(through)),
        out_shape=ATTEND_OUT + tuple(shape(t.shape, t.dtype) for t in through),
        in_specs=[SM] * 2
        + [VM, HB, VM, VM, VM, HB, VM]
        + [HB] * (2 + len(after) + len(through))
        + ([HB] * n if again else []),
        out_specs=(HB,) * (n + len(through)),
        scratch_shapes=[pltpu.VMEM(o.shape, o.dtype) for o in ATTEND_HELD]
        + [
            pltpu.VMEM(proj_in.shape, BF),
            pltpu.VMEM(proj_out.shape, BF),
            pltpu.VMEM(kept[0].shape, BF),
            pltpu.VMEM(kept[4].shape, F32),
            pltpu.VMEM((ROWS, ROWS), F32),
            pltpu.VMEM((ROWS, WIDTH), BF),
            pltpu.SemaphoreType.DMA((4,)),
            pltpu.SemaphoreType.DMA((n,)),
        ],
        input_output_aliases=aliases,
        compiler_params=pltpu.CompilerParams(vmem_limit_bytes=BIG),
        cost_estimate=pl.CostEstimate(flops=5 * 10**9, bytes_accessed=15 * 10**6, transcendentals=0),
    )(*given, *through, *(earlier if again else ()))
    return found[:n], found[n:]


def gate_kernel(first, passed, top_grad, *refs):
    refs[-1][...] = jnp.where(first[0] == 1, passed[...].astype(F32), top_grad[...].astype(F32)).astype(BF)


def gate(first, passed, top_grad, after):
    return pl.pallas_call(
        gate_kernel,
        out_shape=shape(passed.shape, BF),
        in_specs=[SM, VM, VM] + [HB] * len(after),
        out_specs=VM,
    )(first, passed, top_grad, *after)


TERMS = WIDTH + KEYS + HEADS


def pool_back_kernel(
    after,
    grad,
    pool_w,
    patch,
    prob,
    value_t,
    table_hbm,
    value_hbm,
    key_hbm,
    probe,
    *refs,
):
    out, line, mixed_t, blend, values, scores, table, value_w, key_w, sem = refs[after:]
    copies = [
        pltpu.make_async_copy(source, target, sem.at[i])
        for i, (source, target) in enumerate(
            ((table_hbm, table), (value_hbm, value_w), (key_hbm, key_w))
        )
    ]
    for copy in copies:
        copy.start()
    mixed_t[...] = dot(pool_w[...], grad[...].astype(BF), NT).astype(BF)
    lane = lax.broadcasted_iota(jnp.int32, (VARS, HEADS), 1)

    def head(h, c):
        rows = span(h, HEAD)
        back = dot(value_t[rows, :], mixed_t[rows, :], TN)
        grad_prob = back[PIX * VARS :]
        for p in range(PIX):
            grad_prob = grad_prob + back[p * VARS : (p + 1) * VARS] * patch[p]
        weight = prob[h]
        inner = jnp.sum(grad_prob * weight, axis=0, keepdims=True)
        grad_score = (weight * (grad_prob - inner)).astype(BF).astype(F32)
        for p in range(PIX + 1):
            lines = slice(p * VARS, (p + 1) * VARS)
            seen = grad_score if p == PIX else grad_score * patch[p]
            total = jnp.sum(seen, axis=-1, keepdims=True) * 0.125
            scores[lines] = jnp.where(lane == h, total, scores[lines])
            blend[lines] = (weight if p == PIX else weight * patch[p]).astype(BF)
        values[rows, :] = dot(mixed_t[rows, :], blend[...], NT).astype(BF)
        return c

    scores[...] = jnp.zeros_like(scores)
    lax.fori_loop(0, HEADS, head, 0, unroll=8)
    score = scores[...].astype(BF)
    for copy in copies:
        copy.wait()
    out[:, :WIDTH] = dot(table[...], values[...], ((0,), (1,))).astype(BF)
    embed = dot(value_w[...], values[...], NN) + dot(probe[...].astype(BF), score, ((0,), (1,)))
    probe_term = dot(table[...], score, TN)
    out[:, WIDTH:] = jnp.concatenate([embed, probe_term], axis=1).astype(BF)
    crossed = dot(probe_term.astype(BF), key_w[...], TN)
    row = lax.broadcasted_iota(jnp.int32, (HEADS, WIDTH), 0)
    col = lax.broadcasted_iota(jnp.int32, (HEADS, WIDTH), 1)
    line[...] = jnp.sum(jnp.where(col // HEAD == row, crossed, 0.0), axis=0, keepdims=True)


def pool_back(grad, pool_w, patch, prob, value_t, table, value_w, key_w, probe, after):
    return pl.pallas_call(
        partial(pool_back_kernel, len(after)),
        out_shape=(shape((WIDTH, TERMS), BF), shape((1, WIDTH), F32)),
        in_specs=[VM] * 5 + [HB] * 3 + [VM] + [HB] * len(after),
        out_specs=(VM, VM),
        scratch_shapes=[
            pltpu.VMEM((WIDTH, ROWS), BF),
            pltpu.VMEM((KEYS, ROWS), BF),
            pltpu.VMEM((WIDTH, KEYS), BF),
            pltpu.VMEM((KEYS, HEADS), F32),
            pltpu.VMEM(table.shape, BF),
            pltpu.VMEM(value_w.shape, BF),
            pltpu.VMEM(key_w.shape, BF),
            pltpu.SemaphoreType.DMA((3,)),
        ],
        compiler_params=pltpu.CompilerParams(vmem_limit_bytes=BIG),
        cost_estimate=pl.CostEstimate(flops=3 * 10**9, bytes_accessed=12 * 10**6, transcendentals=0),
    )(grad, pool_w, patch, prob, value_t, table, value_w, key_w, probe, *after)


def scatter_rows(stage, slots, block, value, axis):
    if axis == 2:
        stage[slots[block]] = value
    elif axis == 1:
        for y in range(SIDE):
            stage[slots[y], pl.ds(block * 64, 64), :] = value[y * 64 : (y + 1) * 64]
    else:
        for y in range(SIDE):
            for x in range(SIDE):
                at = y * 64 + x * 16
                stage[slots[x], pl.ds(block * 64 + y * 16, 16), :] = value[at : at + 16]


def term_kernel(count, offsets, axis, extra, tail, after, slots, *refs):
    left = refs[:count]
    right = [refs[count * (i + 1) : count * (i + 2)] for i in range(len(offsets))]
    refs = refs[count * (len(offsets) + 1) :]
    if extra:
        more, refs = refs[0], refs[1:]
    if tail:
        small, refs = refs[0], refs[1:]
    refs = refs[after:]
    outs, (stage, sem) = refs[:SIDE], refs[SIDE:]
    own = [slots[axis * SIDE + i] for i in range(SIDE)]
    for block in range(SIDE):
        made = []
        for parts, (base, first, size) in zip(right, offsets):
            total = None
            for a, b in zip(left, parts):
                got = dot(
                    a[:, base + block * 256 : base + (block + 1) * 256],
                    b[:, first : first + size],
                    TN,
                )
                total = got if total is None else total + got
            made.append(total.astype(BF))
        if extra:
            made.append(more[block * 256 : (block + 1) * 256, extra[0] : extra[1]])
        made = made[0] if len(made) == 1 else jnp.concatenate(made, axis=1)
        scatter_rows(stage, own, block, made, axis)
    if tail:
        for k in range(SIDE):
            stage[k, WIDTH // SIDE :, :WIDTH] = small[...]
            stage[k, WIDTH // SIDE :, WIDTH:] = jnp.zeros((tail, stage.shape[2] - WIDTH), BF)
    copies = [pltpu.make_async_copy(stage.at[k], outs[k], sem.at[k]) for k in range(SIDE)]
    for c in copies:
        c.start()
    for c in copies:
        c.wait()


def weight_term(
    slots, left, rights, offsets, axis, extra=None, more=None, small=None, after=()
):
    columns = sum(o[2] for o in offsets) + (extra[1] - extra[0] if extra else 0)
    tail = 0 if small is None else small.shape[0]
    out = shape((WIDTH // SIDE + tail, columns), BF)
    given = [*left, *[r for parts in rights for r in parts]]
    given += [more] if extra else []
    given += [small] if tail else []
    return pl.pallas_call(
        partial(term_kernel, len(left), offsets, axis, extra, tail, len(after)),
        out_shape=(out,) * SIDE,
        in_specs=[SM] + [VM] * len(given) + [HB] * len(after),
        out_specs=(HB,) * SIDE,
        scratch_shapes=[pltpu.VMEM((SIDE,) + out.shape, BF), pltpu.SemaphoreType.DMA((SIDE,))],
        compiler_params=pltpu.CompilerParams(vmem_limit_bytes=BIG),
        cost_estimate=pl.CostEstimate(flops=2 * 10**9, bytes_accessed=5 * 10**6, transcendentals=0),
    )(slots, *given, *after)


def add_kernel(axis, inner, tail, slots, a, b, c, d, *refs):
    outs, (stage, sem) = refs[:SIDE], refs[SIDE:]
    rows = a.shape[0] - tail
    part = rows // SIDE
    total = a[...].astype(F32) + b[...].astype(F32) + c[...].astype(F32) + d[...].astype(F32)
    total = total.astype(BF)
    for i in range(SIDE):
        slot = slots[axis * SIDE + i]
        if inner:
            for j in range(SIDE):
                at = (j * SIDE + i) * 16
                stage[slot, j * 16 : (j + 1) * 16, :] = total[at : at + 16]
        else:
            stage[slot, :part, :] = total[i * part : (i + 1) * part]
        if tail:
            stage[slot, part:, :] = total[rows:]
    copies = [pltpu.make_async_copy(stage.at[k], outs[k], sem.at[k]) for k in range(SIDE)]
    for c in copies:
        c.start()
    for c in copies:
        c.wait()


def add_up(slots, pieces, axis, inner, tail=0):
    rows, columns = pieces[0].shape
    out = shape(((rows - tail) // SIDE + tail, columns), BF)
    return pl.pallas_call(
        partial(add_kernel, axis, inner, tail),
        out_shape=(out,) * SIDE,
        in_specs=[SM] + [VM] * 4,
        out_specs=(HB,) * SIDE,
        scratch_shapes=[pltpu.VMEM((SIDE,) + out.shape, BF), pltpu.SemaphoreType.DMA((SIDE,))],
        compiler_params=pltpu.CompilerParams(vmem_limit_bytes=BIG),
        cost_estimate=pl.CostEstimate(flops=10**6, bytes_accessed=5 * 10**6, transcendentals=0),
    )(slots, *pieces)


def last_kernel(order, *refs):
    xs, ys, zs = refs[:4], refs[4:8], refs[8:12]
    query_vec, var_q, query_w = refs[12:15]
    (
        up,
        out,
        down,
        into,
        pool,
        value,
        embed,
        var,
        key,
        qweight,
        vquery,
        line_two,
        line_down,
        line_one,
        line_up,
    ) = refs[15:]
    wide, narrow, third = FF // SIDE, WIDTH // SIDE, 3 * WIDTH // SIDE
    own = up.shape[0]
    total_x = total_z = small = 0.0
    for k in range(SIDE):
        back = (SIDE - k) % SIDE
        q = order[back]
        up[:, span(q, wide)] = xs[k][:own, :wide].astype(F32)
        out[:, span(q, narrow)] = xs[k][:own, wide : wide + narrow].astype(F32)
        q = order[4 + back]
        down[:, span(q, wide)] = ys[k][:, :wide].astype(F32)
        q = order[8 + back]
        into[:, span(q, third)] = zs[k][:, :third].astype(F32)
        pool[:, span(q, narrow)] = zs[k][:, third : third + narrow].astype(F32)
        total_x = total_x + xs[k][:own, wide + narrow :].astype(F32)
        total_z = total_z + zs[k][:, third + narrow :].astype(F32)
        small = small + xs[k][own:, :WIDTH].astype(F32)
    total = jnp.concatenate([total_z, total_x], axis=1)
    value[...] = total[:, :WIDTH]
    for p in range(PIX):
        at = WIDTH + p * VARS
        embed[p] = total[:, at : at + VARS]
    var[...] = total[:, WIDTH + PIX * VARS : WIDTH + KEYS]
    row = lax.broadcasted_iota(jnp.int32, (HEADS, WIDTH), 0)
    col = lax.broadcasted_iota(jnp.int32, (HEADS, WIDTH), 1)
    spread = jnp.where(col // HEAD == row, 1.0, 0.0)
    probe = jnp.dot(
        total[:, WIDTH + KEYS :],
        spread,
        precision=lax.Precision.HIGHEST,
        preferred_element_type=F32,
    )
    key[...] = probe * query_vec[...]
    qvec = small[0:1]
    qweight[...] = var_q[...] * qvec
    exact = partial(
        lax.dot_general, precision=lax.Precision.HIGHEST, preferred_element_type=F32
    )
    vquery[...] = exact(qvec, query_w[...].astype(F32), (NT, ((), ())))
    chip = order[8] * SIDE * SIDE + order[4] * SIDE + order[0]
    row = lax.broadcasted_iota(jnp.int32, (WIDTH, own), 0)
    col = lax.broadcasted_iota(jnp.int32, (WIDTH, own), 1)
    mine = exact(small, jnp.where(row == chip * own + col, 1.0, 0.0), (NN, ((), ())))
    line_two[...] = mine[1:2]
    line_down[...] = mine[2:3]
    line_one[...] = mine[7:8]
    row = lax.broadcasted_iota(jnp.int32, (WIDTH, SIDE * own), 0)
    col = lax.broadcasted_iota(jnp.int32, (WIDTH, SIDE * own), 1)
    first = (chip % (SIDE * SIDE)) * SIDE * own
    mine = exact(small, jnp.where(row == first + col, 1.0, 0.0), (NN, ((), ())))
    row = lax.broadcasted_iota(jnp.int32, mine.shape, 0)
    line_up[...] = jnp.sum(
        jnp.where(row == 3 + order[8], mine, 0.0), axis=0, keepdims=True
    )


def last_step(order, xs, ys, zs, query_vec, var_q, query_w):
    own = WIDTH // SIDE**3
    return pl.pallas_call(
        last_kernel,
        out_shape=(
            shape((own, FF), F32),
            shape((own, WIDTH), F32),
            shape((own, FF), F32),
            shape((own, 3 * WIDTH), F32),
            shape((own, WIDTH), F32),
            shape((own, WIDTH), F32),
            shape((PIX, own, VARS), F32),
            shape((own, VARS), F32),
            shape((own, WIDTH), F32),
            shape((own, WIDTH), F32),
            shape((1, own), F32),
            shape((1, own), F32),
            shape((1, own), F32),
            shape((1, own), F32),
            shape((1, SIDE * own), F32),
        ),
        in_specs=[SM] + [VM] * 15,
        out_specs=(VM,) * 15,
        compiler_params=pltpu.CompilerParams(vmem_limit_bytes=BIG),
    )(order, *xs, *ys, *zs, query_vec, var_q, query_w)


def local(
    tokens,
    pixels,
    segments,
    embed_weight,
    var_embed,
    var_query,
    query_weight,
    key_weight,
    value_weight,
    pool_weight,
    first_gain,
    project_in,
    project_out,
    second_gain,
    up_weight,
    up_bias,
    down_weight,
    down_bias,
    cotangent,
):
    section = lax.axis_index("section")
    is_first = section == 0
    micro, _, seq, width = tokens.shape
    rows = micro * seq
    value_w, query_w, key_w = value_weight[0], query_weight[0], key_weight[0]
    up_w, down_w, proj_in, proj_out, pool_w = (
        w[0] for w in (up_weight, down_weight, project_in, project_out, pool_weight)
    )
    table = jnp.concatenate(
        [embed_weight[0].transpose(1, 0, 2).reshape(PIX * VARS, width), var_embed[0]]
    )
    query_vec, probe, quick, value_t = prepare(table, var_query, query_w, key_w, value_w)
    patch = pixels[:, 0].astype(F32).transpose(2, 1, 0, 3).reshape(PIX, VARS, rows)
    seg_ids = (segments[:, 0] + SIDE * jnp.arange(micro)[:, None]).reshape(rows)
    seg_c, seg_r = seg_ids[:, None], seg_ids[None]
    inputs = tokens.reshape(rows, width)
    on_first = jnp.where(is_first, 1, 0).astype(jnp.int32).reshape(1)
    on_second = 1 - on_first

    sign = jnp.where(is_first, 1, -1)
    steps = jnp.arange(SIDE)
    spots = [place(axis) for axis in "xyz"]
    order = jnp.concatenate([(at + sign * steps) % SIDE for at in spots]).astype(jnp.int32)
    slots = jnp.concatenate([(sign * (steps - at)) % SIDE for at in spots]).astype(jnp.int32)

    base = (patch, seg_c, seg_r, quick, value_t)
    lines = (first_gain, second_gain, up_bias, down_bias)
    weights = (pool_w, proj_in, proj_out, up_w, down_w)
    saved = forward(on_first, order, inputs, base, lines, weights, None)
    passed = lax.ppermute(saved[0], "section", [(0, 1)])
    saved = forward(on_second, order, passed, base, lines, weights, saved)
    result, prob, stream, stream_two, qkv, lse, slope, for_x, for_z = saved[:9]
    hidden = saved[9:]
    kept = (qkv, lse, seg_c, seg_r, stream)

    top_grad = cotangent.reshape(rows, width)
    low = mlp_back(
        on_second, order, top_grad, stream_two, slope, second_gain, up_w, down_w, (), None
    )
    all_x = share(for_x, "x")
    first_z = [swap(for_z, "z", k) for k in (1, 3)]
    high, (for_z, *hidden) = attend_back(
        on_second,
        order,
        low[0],
        kept,
        first_gain,
        proj_in,
        proj_out,
        (*all_x[1:], *first_z),
        None,
        (for_z, *hidden),
    )
    passed = lax.ppermute(high[0].astype(BF), "section", [(1, 0)])
    all_z = [for_z, first_z[0], swap(for_z, "z", 2), first_z[1]]
    all_y = handed(hidden, "y")
    branch_down = gate(on_first, passed, top_grad, (*all_y[1:], all_z[2]))
    down_all = share(branch_down, "y")
    low = mlp_back(
        on_first, order, branch_down, stream_two, slope, second_gain, up_w, down_w, (), low
    )
    high, _ = attend_back(
        on_first, order, low[0], kept, first_gain, proj_in, proj_out, tuple(down_all[1:]), high, ()
    )
    low_lines, grad_pre = low[1], low[2:]
    grad_in, high_lines, grad_qkv = high[0], high[1], high[2:]

    pre_all = handed(grad_pre, "x")
    qkv_all = handed(grad_qkv, "z")
    more, qvec_term = pool_back(
        grad_in, pool_w, patch, prob, value_t, table, value_w, key_w, probe, ()
    )
    small = jnp.concatenate(
        [qvec_term, low_lines[:6], high_lines[:1], jnp.zeros((8, width), F32)]
    ).astype(BF)

    wide, narrow, third = FF // SIDE, WIDTH // SIDE, 3 * WIDTH // SIDE
    half = TERMS // 2
    ys = weight_term(
        slots, down_all, [all_y], ((0, 0, wide),), 2
    )
    xs = weight_term(
        slots,
        all_x,
        [pre_all, pre_all],
        ((0, 0, wide), (WIDTH, wide, narrow)),
        1,
        (half, TERMS),
        more,
        small,
    )
    zs = weight_term(
        slots,
        all_z,
        [qkv_all, qkv_all],
        ((0, 0, third), (WIDTH, third, narrow)),
        0,
        (0, half),
        more,
        after=(),
    )
    tail = small.shape[0]
    ys = add_up(slots, handed(ys, "z"), 0, True)
    xs = add_up(slots, handed(xs, "y"), 2, False, tail)
    zs = add_up(slots, handed(zs, "x"), 1, True)
    ys = add_up(slots, handed(ys, "x"), 1, False)
    xs = add_up(slots, handed(xs, "z"), 0, False, tail)
    zs = add_up(slots, handed(zs, "y"), 2, False)
    own = width // SIDE**3
    at = lax.axis_index("batch") * own
    mine = partial(lax.dynamic_slice_in_dim, start_index=at, slice_size=own)
    (
        grad_up,
        grad_out,
        grad_down,
        grad_in_w,
        grad_pool,
        grad_value,
        grad_embed,
        grad_var,
        grad_key,
        grad_qw,
        grad_vq,
        line_two,
        line_down,
        line_one,
        line_up,
    ) = last_step(
        order,
        handed(xs, "x"),
        handed(ys, "y"),
        handed(zs, "z"),
        query_vec,
        mine(var_query[0], axis=0).astype(F32)[:, None],
        mine(query_w, axis=0),
    )
    grad_embed = grad_embed.transpose(2, 0, 1)
    grad_var = grad_var.T
    grad_down = grad_down.T

    return (
        result.reshape(1, micro, 1, seq, width),
        grad_in.reshape(1, micro, 1, seq, width),
        grad_embed[None],
        grad_var[None],
        grad_vq,
        grad_qw[None],
        grad_key[None],
        grad_value[None],
        grad_pool[None],
        line_one,
        grad_in_w[None],
        grad_out[None],
        line_two,
        grad_up[None],
        line_up,
        grad_down[None],
        line_down,
    )


def solution(mesh):
    in_specs = (
        P(None, "batch", None, None),
        P(None, "batch", None, None, None),
        P(None, "batch", None),
        P("section", None, None, None),
        P("section", None, None),
        P("section", None),
        P("section", None, None),
        P("section", None, None),
        P("section", None, None),
        P("section", None, None),
        P("section", None),
        P("section", None, None),
        P("section", None, None),
        P("section", None),
        P("section", None, None),
        P("section", None),
        P("section", None, None),
        P("section", None),
        P(None, "batch", None, None),
    )
    out_specs = (
        P("section", None, "batch", None, None),
        P("section", None, "batch", None, None),
        P("section", None, None, "batch"),
        P("section", None, "batch"),
        P("section", "batch"),
        P("section", "batch", None),
        P("section", "batch", None),
        P("section", "batch", None),
        P("section", "batch", None),
        P("section", "batch"),
        P("section", "batch", None),
        P("section", "batch", None),
        P("section", "batch"),
        P("section", "batch", None),
        P("section", "batch"),
        P("section", None, "batch"),
        P("section", "batch"),
    )
    return jax.shard_map(local, mesh=mesh, in_specs=in_specs, out_specs=out_specs, check_vma=False)
```
